32 devices in a mesh: rel: 4 (over y, x), node: 8 (over z, core).
Axes of the slice: x: 2, y: 2, z: 4, core: 2. Of those that a mesh axis runs over, the one named last changes fastest.
Arguments:
- out_adjoint: bfloat16 [8, 1024, 512], P('node', 'rel'), may hold values from -6 to 6
- layer_input: bfloat16 [8, 1024, 512], P('node'), may hold values from -0.15625 to 0.15625
- rel_weights: bfloat16 [8, 512, 512], P('rel'), may hold values from -0.25 to 0.25
- self_weight: bfloat16 [512, 512], replicated, may hold values from -0.25 to 0.25
- tile_values: bfloat16 [4, 256, 128, 128], P('rel', 'node'), may hold values from 0 to 0.039794922
- tile_rel: int32 [4, 256], P('rel', 'node'), may hold values from 0 to 1
- tile_target: int32 [4, 256], P('rel', 'node'), may hold values from 0 to 7
- tile_src: int32 [4, 256], P('rel', 'node'), may hold values from 0 to 7
- tile_dest: int32 [4, 256, 1], P('rel', 'node'), may hold values from 0 to 7; in each aligned block of 32 rows (0 to 31, 32 to 63, ..., all dimensions but the last counted through in order) at most 8 rows name the same one
Outputs:
- rel_weight_grad: float32 [8, 512, 512], P('rel', 'node')
- d_source: bfloat16 [8, 1024, 512], P('node', 'rel')
The draws below stay inside these ranges and needn't reach their ends.
Inputs may be any that keep to these rules, and one draw needn't show every extreme that they name: `tile_dest`: among the 32 tiles of one device, at most 8 name the same node shard, and some node shard is named by exactly 8 of them.
All inputs are finite; a program needn't handle non-finite values.
Results may differ from the reference program's by a relative error of at most 0.0056.
Values may be sent and summed in bfloat16 or wider, within the bound.
No kernel may reach another device: no remote copies, remote signals or barrier semaphores. Data moves between devices by JAX's collectives and lax.ppermute only.
A program may use at most 128 MiB of HBM per device.

```python
import math
import jax
import jax.numpy as jnp
import numpy as np
from jax import lax

D = 512
TB = 128
ROWS_DEV = 1024
REL_DEV = 2
BLOCKS = 8
CAP = 8
TILES_DEV = 32
RELS = 8
NODES = 8192
N_REL = 4
N_NODE = 8


def plant(drawn, own_key, smallest, largest):
    longest = drawn.shape.index(max(drawn.shape))
    spots = []
    for shift in (0, 1):
        where = [jax.random.randint(jax.random.fold_in(own_key, axis), (), 0, length) for axis, length in enumerate(drawn.shape)]
        where[longest] = (where[longest] + shift) % drawn.shape[longest]
        spots.append(tuple(where))
    return drawn.at[spots[0]].set(smallest).at[spots[1]].set(largest)


def strengthened(drawn, own_key, source, target, parts, factor):
    owner, partner = [(jnp.arange(drawn.shape[position]) // (drawn.shape[position] // parts)).reshape([-1 if axis == position else 1 for axis in range(drawn.ndim)]) for position in (source, target)]
    chosen = jax.random.permutation(own_key, parts)[partner]
    strong = (owner == chosen) | (owner == (partner + parts // 2) % parts)
    return jnp.where(strong, factor * drawn, drawn)


def shard_levels(rng, shape, split, smallest, high):
    def one(position, parts):
        heights = jax.random.uniform(jax.random.fold_in(jax.random.fold_in(rng, 6), position), (parts,), jnp.float32, smallest / len(split), high / len(split))
        return jnp.repeat(jnp.exp(heights), shape[position] // parts).reshape((-1,) + (1,) * (len(shape) - position - 1))

    loudness = one(*split[0])
    for cut in split[1:]:
        loudness = loudness * one(*cut)
    return loudness


def deal_out(own_key, own, number, rows, amount, top, bound, skew):
    ranking = jax.random.permutation(own_key, amount)
    crowded, usual = shares(amount, rows * top, bound, skew, True), shares(amount, rows * top, bound, skew, False)
    places = jnp.arange(amount)

    def named(sizes, turn):
        used = int((sizes > 0).sum())
        fixed = max(1, used // 4)
        moved = fixed + (places - fixed + turn * (used - fixed)) % max(1, amount - fixed)
        return jnp.zeros((amount,), jnp.int32).at[ranking[jnp.where(places < fixed, places, moved)]].set(jnp.asarray(sizes, jnp.int32))

    sizes = jnp.where(number % 4 == 0, named(crowded, number // 4), named(usual, number - number // 4 - 1))
    mixed = jax.random.permutation(jax.random.fold_in(own, 3), amount)
    source_of, receiver = mixed[0:amount // 2 * 2:2], mixed[1:amount // 2 * 2:2]
    room = jnp.minimum(sizes[source_of] - 1, bound - sizes[receiver]) // 2
    room = jnp.where((source_of == ranking[0]) | (receiver == ranking[0]) | (sizes[receiver] == 0), 0, jnp.maximum(room, 0))
    moved = jax.random.randint(jax.random.fold_in(own, 4), (amount // 2,), 0, 1 << 20) % (room + 1)
    sizes = sizes.at[source_of].add(-moved).at[receiver].add(moved)
    items = jnp.searchsorted(jnp.cumsum(sizes), jnp.arange(rows * top), side="right").astype(jnp.int32)
    grid = items.reshape(top, rows).T
    grid = grid[jax.random.permutation(jax.random.fold_in(own, 1), rows)]
    turn = jax.random.randint(jax.random.fold_in(own, 2), (rows, 1), 0, top)
    return jnp.take_along_axis(grid, (jnp.arange(top)[None, :] + turn) % top, axis=1)


def shares(number_of, total, reach, lean, full):
    loads = [(1 << 20) // math.isqrt(grade ** lean) + 1 for grade in range(1, number_of + 1)]
    largest = reach if full else min(reach, max(-(-total // number_of), total * loads[0] // sum(loads)))
    least = 1 if total - largest >= number_of - 1 else 0
    holding, rest = [largest] + [least] * (number_of - 1), total - largest - least * (number_of - 1)
    while rest > 0:
        free = [i for i in range(1, number_of) if holding[i] < largest] or [i for i in range(1, number_of) if holding[i] < reach]
        whole, left = sum([loads[i] for i in free]), rest
        for i in free:
            addition = min(reach - holding[i], max(1, left * loads[i] // whole), rest)
            holding[i] = holding[i] + addition
            rest = rest - addition
    return np.array(holding)


def centred(rng, dims, spread, reach, split=(), dtype=jnp.bfloat16):
    gain = shard_levels(rng, dims, split, -0.22, 0.18) if split else 1.0
    values = jax.random.normal(rng, dims, jnp.float32) * spread * gain
    return jnp.minimum(jnp.maximum(values, -reach), reach).astype(dtype)


def bell_draw_with(own_key, dims, deviation, reach, pieces, heavy, held_as=jnp.bfloat16):
    entries = deviation * jax.random.normal(own_key, dims, jnp.float32)
    if pieces:
        entries = entries * shard_levels(own_key, dims, pieces, -0.22, 0.18)
    return jnp.clip(strengthened(entries, jax.random.fold_in(own_key, 3), *heavy), -reach, reach).astype(held_as)


def setup_inputs(seed: int = 0) -> dict:
    splits = jax.random.split(jax.random.key(seed), 10)
    out_adjoint = centred(splits[0], (N_NODE, ROWS_DEV, D), 1.0, 6.0, ((0, 8), (1, 4)))
    layer_input = bell_draw_with(splits[1], (N_NODE, ROWS_DEV, D), 0.02, 0.15625, ((0, 8),), (0, 2, 8, 2.0))
    rel_weights = centred(splits[2], (RELS, D, D), D ** -0.5, 0.25, ((0, 4),))
    self_weight = centred(splits[3], (D, D), D ** -0.5, 0.25)
    tile_values = jnp.clip(0.039794922 * jax.random.uniform(splits[4], (N_REL, N_NODE * TILES_DEV, TB, TB), jnp.float32) ** shard_levels(splits[4], (N_REL, N_NODE * TILES_DEV, TB, TB), ((0, 4), (1, 8)), -0.2, 0.2), 0.0, 0.039794922).astype(jnp.bfloat16)
    tile_rel = plant(jax.random.randint(splits[5], (N_REL, N_NODE * TILES_DEV), 0, REL_DEV), jax.random.fold_in(splits[5], 1), 0, REL_DEV - 1).astype(jnp.int32)
    tile_target = plant(jax.random.randint(splits[6], (N_REL, N_NODE * TILES_DEV), 0, BLOCKS), jax.random.fold_in(splits[6], 1), 0, BLOCKS - 1).astype(jnp.int32)
    tile_src = plant(jax.random.randint(splits[7], (N_REL, N_NODE * TILES_DEV), 0, BLOCKS), jax.random.fold_in(splits[7], 1), 0, BLOCKS - 1).astype(jnp.int32)
    tile_dest_keys = jax.random.split(jax.random.fold_in(splits[8], 1), N_REL * (N_NODE * TILES_DEV) // TILES_DEV)
    tile_dest_turns = jax.random.permutation(jax.random.fold_in(splits[8], 3), N_REL * (N_NODE * TILES_DEV) // TILES_DEV)
    tile_dest = jax.vmap(lambda own, number: deal_out(jax.random.fold_in(splits[8], 2), own, number, TILES_DEV, N_NODE, 1, CAP, 2))(tile_dest_keys, tile_dest_turns).reshape((N_REL, N_NODE * TILES_DEV, 1))
    return dict(out_adjoint=out_adjoint, layer_input=layer_input, rel_weights=rel_weights, self_weight=self_weight, tile_values=tile_values, tile_rel=tile_rel, tile_target=tile_target, tile_src=tile_src, tile_dest=tile_dest)


def reference(out_adjoint, layer_input, rel_weights, self_weight, tile_values, tile_rel, tile_target, tile_src, tile_dest):
    adjoint_blocks = out_adjoint.reshape(N_NODE * BLOCKS, TB, D)
    inputs = layer_input.reshape(NODES, D).astype(jnp.float32)
    owners = tile_dest[..., 0]
    sender = (jnp.arange(N_NODE * TILES_DEV) // TILES_DEV).astype(jnp.int32)
    weights_grouped = rel_weights.reshape(N_REL, REL_DEV, D, D)

    def one_group(carry, per_group):
        values, relation, target, source, owner, weights = per_group
        chosen = adjoint_blocks[(sender * BLOCKS + target).astype(jnp.int32)].astype(jnp.float32)
        partial_value = jnp.einsum("tij,tid->tjd", values.astype(jnp.float32), chosen).astype(jnp.bfloat16)
        partial_value = lax.optimization_barrier(partial_value)
        bucket = (relation * (N_NODE * BLOCKS) + owner * BLOCKS + source).astype(jnp.int32)
        summed = jax.ops.segment_sum(partial_value.astype(jnp.float32), bucket, num_segments=REL_DEV * N_NODE * BLOCKS)
        rounded = summed.reshape(REL_DEV, NODES, D).astype(jnp.bfloat16)
        rounded = lax.optimization_barrier(rounded)
        aggregated = rounded.astype(jnp.float32)
        grads = jnp.einsum("vi,rvj->rij", inputs, aggregated)
        carry = carry + jnp.einsum("rvj,rij->vi", aggregated, weights.astype(jnp.float32))
        return carry, grads

    start = jnp.dot(out_adjoint.reshape(NODES, D), self_weight.T, preferred_element_type=jnp.float32)
    total, grads = lax.scan(one_group, start, (tile_values, tile_rel, tile_target, tile_src, owners, weights_grouped))
    return grads.reshape(RELS, D, D), total.astype(jnp.bfloat16).reshape(N_NODE, ROWS_DEV, D)
```

```python
import functools

import jax
import jax.numpy as jnp
from jax import lax
from jax.experimental import pallas as pl
from jax.experimental.pallas import tpu as pltpu
from jax.sharding import PartitionSpec as P

CAPACITY = 8
CORES = 2


def place_kernel(chips, slots, dest_ref, place_ref, tiles_ref, *refs):
    outs, (order, count, sem) = refs[: chips - 1], refs[chips - 1 :]
    chip = place_ref[0]
    for j in range(chips):
        count[j] = 0
    for s in range(chips * slots):
        order[s] = 0

    def rank(t, carry):
        j = (dest_ref[t] // CORES) ^ chip
        p = count[j]
        order[j * slots + p] = t
        count[j] = p + 1
        return carry

    lax.fori_loop(0, dest_ref.shape[0], rank, 0)
    for j in range(chips - 1, 0, -1):
        for p in range(slots):
            pltpu.make_async_copy(
                tiles_ref.at[order[j * slots + p]], outs[j - 1].at[p], sem.at[j - 1]
            ).start()
    for j in range(chips - 1, 0, -1):
        pltpu.make_async_copy(outs[j - 1], outs[j - 1], sem.at[j - 1]).wait()


def place_tiles(dest, place, tiles, chips, slots):
    edge = tiles.shape[-1]
    return pl.pallas_call(
        functools.partial(place_kernel, chips, slots),
        out_shape=[jax.ShapeDtypeStruct((slots, edge, edge), tiles.dtype)] * (chips - 1),
        in_specs=[
            pl.BlockSpec(memory_space=pltpu.SMEM),
            pl.BlockSpec(memory_space=pltpu.SMEM),
            pl.BlockSpec(memory_space=pl.ANY),
        ],
        out_specs=[pl.BlockSpec(memory_space=pl.ANY)] * (chips - 1),
        scratch_shapes=[
            pltpu.SMEM((chips * slots,), jnp.int32),
            pltpu.SMEM((chips,), jnp.int32),
            pltpu.SemaphoreType.DMA((chips - 1,)),
        ],
        cost_estimate=pl.CostEstimate(
            flops=0, bytes_accessed=4 * (chips - 1) * slots * edge * edge, transcendentals=0
        ),
        name="place_tiles",
    )(dest, place, tiles)


def main_kernel(chips, groups, blocks, relations, *refs):
    meta_ref, count_ref, place_ref, own_ref = refs[:4]
    refs = refs[4:]
    sent, refs = refs[: chips - 1], refs[chips - 1 :]
    pieces, refs = refs[: chips * groups], refs[chips * groups :]
    inputs_ref, weights_ref = refs[:2]
    grad_far, grad_own, rows_far, rows_own = refs[2:6]
    adjoint, own_tiles, sent_tiles, total, sem = refs[6:]
    chip, group, core = place_ref[0], place_ref[1], place_ref[2]
    edge = own_ref.shape[-1]
    feature = adjoint.shape[-1]
    piece = pieces[0].shape[0]
    span = relations * blocks

    def copies(j):
        out = []
        for m in range(groups):
            row = pl.multiple_of((group ^ m) * piece, piece)
            out.append(
                pltpu.make_async_copy(
                    pieces[j * groups + m], adjoint.at[j, pl.ds(row, piece)], sem.at[j, m]
                )
            )
        if j == 0:
            out.append(pltpu.make_async_copy(own_ref, own_tiles, sem.at[j, groups]))
        else:
            out.append(
                pltpu.make_async_copy(sent[j - 1], sent_tiles.at[j - 1], sem.at[j, groups])
            )
        return out

    for j in range(chips):
        for copy in copies(j):
            copy.start()
    total[...] = jnp.zeros_like(total)
    for j in range(chips):
        for copy in copies(j):
            copy.wait()

        def one(p, carry):
            code = meta_ref[j, p]
            bucket = code % (CORES * span)
            rest = code // (CORES * span)
            row = pl.multiple_of((rest % blocks) * edge, edge)
            tile = own_tiles[rest // blocks] if j == 0 else sent_tiles[j - 1, p]
            partial = lax.dot_general(
                tile,
                adjoint[j, pl.ds(row, edge), :],
                (((0,), (0,)), ((), ())),
                preferred_element_type=jnp.float32,
            )
            total[bucket] += partial.astype(jnp.bfloat16).astype(jnp.float32)
            return carry

        lax.fori_loop(0, count_ref[j], one, 0)

    rows = blocks * edge
    share = feature // (chips * CORES)
    for r in range(relations):
        grad = jnp.zeros((feature, feature), jnp.float32)
        for h in range(CORES):
            part = total[pl.ds((h * relations + r) * blocks, blocks)].astype(jnp.bfloat16)
            grad += jnp.dot(
                inputs_ref[h], part.reshape(rows, feature), preferred_element_type=jnp.float32
            )
        for far in range(CORES):
            out = grad_far if far else grad_own
            for c in range(chips):
                for h in range(CORES):
                    piece_of = grad[(c * CORES + h) * share : (c * CORES + h + 1) * share]

                    @pl.when(h == (core ^ far))
                    def _():
                        out[chip ^ c, r] = piece_of.astype(out.dtype)

    for h in range(CORES):
        value = jnp.zeros((rows, feature), jnp.float32)
        for r in range(relations):
            part = total[pl.ds((h * relations + r) * blocks, blocks)].astype(jnp.bfloat16)
            value += lax.dot_general(
                part.reshape(rows, feature),
                weights_ref[r],
                (((1,), (1,)), ((), ())),
                preferred_element_type=jnp.float32,
            )
        for far in range(CORES):
            out = rows_far if far else rows_own

            @pl.when(h == (core ^ far))
            def _():
                for q in range(groups):
                    out[group ^ q] = value[q * piece : (q + 1) * piece].astype(out.dtype)


def main(meta, count, place, own_tiles, sent, pieces, inputs, weights, chips, groups, blocks):
    edge = own_tiles.shape[-1]
    relations, feature = weights.shape[0], weights.shape[-1]
    slots = meta.shape[1]
    piece = pieces[0].shape[0]
    share = feature // (chips * CORES)
    rows = blocks * edge
    smem = pl.BlockSpec(memory_space=pltpu.SMEM)
    hbm = pl.BlockSpec(memory_space=pl.ANY)
    vmem = pl.BlockSpec(memory_space=pltpu.VMEM)
    return pl.pallas_call(
        functools.partial(main_kernel, chips, groups, blocks, relations),
        out_shape=[
            jax.ShapeDtypeStruct((chips, relations, share, feature), jnp.bfloat16),
            jax.ShapeDtypeStruct((chips, relations, share, feature), jnp.float32),
            jax.ShapeDtypeStruct((groups, piece, feature), jnp.bfloat16),
            jax.ShapeDtypeStruct((groups, piece, feature), jnp.float32),
        ],
        in_specs=[smem, smem, smem, hbm] + [hbm] * (len(sent) + len(pieces)) + [vmem, vmem],
        out_specs=[vmem] * 4,
        scratch_shapes=[
            pltpu.VMEM((chips, rows, feature), jnp.bfloat16),
            pltpu.VMEM(own_tiles.shape, jnp.bfloat16),
            pltpu.VMEM((chips - 1, slots, edge, edge), jnp.bfloat16),
            pltpu.VMEM((CORES * relations * blocks, edge, feature), jnp.float32),
            pltpu.SemaphoreType.DMA((chips, groups + 1)),
        ],
        compiler_params=pltpu.CompilerParams(vmem_limit_bytes=44 * 1024 * 1024),
        cost_estimate=pl.CostEstimate(
            flops=8 * rows * feature * feature, bytes_accessed=20_000_000, transcendentals=0
        ),
        name="tiles_and_products",
    )(meta, count, place, own_tiles, *sent, *pieces, inputs, weights)


def on_device(
    out_adjoint,
    layer_input,
    rel_weights,
    self_weight,
    tile_values,
    tile_rel,
    tile_target,
    tile_src,
    tile_dest,
):
    nodes = lax.axis_size("node")
    groups = lax.axis_size("rel")
    chips = nodes // CORES
    node = lax.axis_index("node")
    group = lax.axis_index("rel")
    chip, core = node // CORES, node % CORES
    edge = tile_values.shape[-1]
    rows = layer_input.shape[1]
    feature = layer_input.shape[2]
    blocks = rows // edge
    relations = rel_weights.shape[0]
    tiles = tile_values.shape[1]
    slots = CORES * CAPACITY

    def across(value, axis, size, mask):
        return lax.ppermute(value, axis, [(i, i ^ mask) for i in range(size)])

    def to_chip(value, j):
        return across(value, "node", nodes, CORES * j)

    own = out_adjoint[0]
    place = jnp.stack([chip, group, core]).astype(jnp.int32)
    dest = tile_dest[0, :, 0]

    by_chip = {0: own}
    bit = chips // 2
    while bit:
        for j in list(by_chip):
            by_chip[j ^ bit] = to_chip(by_chip[j], bit)
        bit //= 2
    sent = place_tiles(dest, place, tile_values[0], chips, slots)
    sent = [to_chip(sent[j - 1], j) for j in range(1, chips)]
    pieces = []
    for j in range(chips):
        pieces.append(by_chip[j])
        for m in range(1, groups):
            pieces.append(across(by_chip[j], "rel", groups, m))

    index = jnp.arange(tiles, dtype=jnp.int32)
    code = (index * blocks + tile_target[0]) * (CORES * relations * blocks) + (
        (dest % CORES) * relations + tile_rel[0]
    ) * blocks + tile_src[0]
    gathered = lax.all_gather(jnp.stack([dest // CORES, code]), "node", axis=0)
    gathered = gathered.reshape(chips, CORES, 2, tiles)
    gathered = lax.dynamic_index_in_dim(gathered, core, 1, keepdims=False)
    turned = (jnp.arange(chips)[:, None] ^ chip) == jnp.arange(chips)[None, :]
    gathered = jnp.sum(jnp.where(turned[:, :, None, None], gathered[None], 0), axis=1)
    mine = gathered[:, 0] == chip
    rank = jnp.sum(
        jnp.where(mine[:, None, :] & (index[None, :] < index[:, None])[None], 1, 0), axis=2
    )
    chosen = mine[:, None, :] & (rank[:, None, :] == jnp.arange(slots)[None, :, None])
    meta = jnp.sum(jnp.where(chosen, gathered[:, 1][:, None, :], 0), axis=2).astype(jnp.int32)
    count = jnp.sum(mine, axis=1).astype(jnp.int32)

    near = layer_input[0]
    far = across(near, "node", nodes, 1)
    inputs = jnp.stack([jnp.where(core == 0, near, far), jnp.where(core == 0, far, near)])
    inputs = jnp.swapaxes(inputs, 1, 2)

    grad_far, grad_own, rows_far, rows_own = main(
        meta, count, place, tile_values[0], sent, pieces, inputs, rel_weights, chips, groups, blocks
    )
    grad_far = across(grad_far, "node", nodes, 1)
    rows_far = across(rows_far, "node", nodes, 1)
    grad = grad_own + grad_far.astype(jnp.float32)
    others = [to_chip(grad[j].astype(jnp.bfloat16), j) for j in range(1, chips)]
    rel_weight_grad = grad[0]
    for other in others:
        rel_weight_grad += other.astype(jnp.float32)

    totals = rows_own + rows_far.astype(jnp.float32)
    others = [
        across(totals[m].astype(jnp.bfloat16), "rel", groups, m) for m in range(1, groups)
    ]
    d_source = totals[0] + jnp.einsum(
        "vj,ij->vi", own, self_weight, preferred_element_type=jnp.float32
    )
    for other in others:
        d_source += other.astype(jnp.float32)
    return rel_weight_grad, d_source.astype(jnp.bfloat16)[None]


def solution(mesh):
    return jax.shard_map(
        on_device,
        mesh=mesh,
        in_specs=(
            P("node", "rel", None),
            P("node", None, None),
            P("rel", None, None),
            P(),
            P("rel", "node", None, None),
            P("rel", "node"),
            P("rel", "node"),
            P("rel", "node"),
            P("rel", "node", None),
        ),
        out_specs=(P("rel", "node", None), P("node", "rel", None)),
        check_vma=False,
    )
```

```python
import functools

import jax
import jax.numpy as jnp
from jax import lax
from jax.experimental import pallas as pl
from jax.experimental.pallas import tpu as pltpu
from jax.sharding import PartitionSpec as P

CAPACITY = 8
CORES = 2
SLOTS = CORES * CAPACITY
LIMIT = 32 * 1024 * 1024
HEAD = 5
SMEM = pl.BlockSpec(memory_space=pltpu.SMEM)
VMEM = pl.BlockSpec(memory_space=pltpu.VMEM)
ANY = pl.BlockSpec(memory_space=pl.ANY)


def payload_rows(edge, first, size):
    return size * edge + (SLOTS if first == 0 else 0)


def place_kernel(parts, chips, blocks, relations, *refs):
    given, place_ref, outs = refs[:2], refs[2], refs[3 : 3 + len(parts)]
    details, tiles_ref, order, count, sem = refs[3 + len(parts) :]
    copies = [
        pltpu.make_async_copy(given[0], details, sem.at[0]),
        pltpu.make_async_copy(given[1], tiles_ref, sem.at[1]),
    ]
    for copy in copies:
        copy.start()
    chip = place_ref[0]
    edge = tiles_ref.shape[-1]
    for j in range(chips):
        count[j] = 0
    for s in range(chips * SLOTS):
        order[s] = 0
    copies[0].wait()

    def rank(t, carry):
        j = (details[0, t] // CORES) ^ chip
        p = count[j]
        order[j * SLOTS + p] = t
        count[j] = p + 1
        return carry

    lax.fori_loop(0, details.shape[1], rank, 0)
    copies[1].wait()
    lane = lax.broadcasted_iota(jnp.int32, (SLOTS, edge), 1)
    row = lax.broadcasted_iota(jnp.int32, (SLOTS, edge), 0)
    for out, (j, first, size) in zip(outs, parts, strict=True):
        for p in range(size):
            tile = tiles_ref[order[j * SLOTS + first + p]]
            full = first + p < count[j]
            out[p * edge : (p + 1) * edge, :] = jnp.where(full, tile, jnp.zeros_like(tile))
        if first == 0:
            codes = jnp.zeros((SLOTS, edge), jnp.int32)
            for p in range(SLOTS):
                t = order[j * SLOTS + p]
                bucket = (details[0, t] % CORES) * relations + details[1, t]
                code = jnp.where(lane == 0, bucket * blocks + details[3, t], details[2, t])
                codes = jnp.where(row == p, code, codes)
            out[size * edge :, :] = codes.astype(jnp.float32).astype(jnp.bfloat16)


def place_tiles(parts, chips, blocks, relations, details, tiles, place):
    edge = tiles.shape[-1]
    shapes = [
        jax.ShapeDtypeStruct((payload_rows(edge, first, size), edge), tiles.dtype)
        for _, first, size in parts
    ]
    return pl.pallas_call(
        functools.partial(place_kernel, parts, chips, blocks, relations),
        out_shape=shapes,
        in_specs=[ANY] * 2 + [SMEM],
        out_specs=[VMEM] * len(shapes),
        scratch_shapes=[
            pltpu.SMEM(details.shape, jnp.int32),
            pltpu.VMEM(tiles.shape, tiles.dtype),
            pltpu.SMEM((chips * SLOTS,), jnp.int32),
            pltpu.SMEM((chips,), jnp.int32),
            pltpu.SemaphoreType.DMA((2,)),
        ],
        compiler_params=pltpu.CompilerParams(vmem_limit_bytes=LIMIT),
        cost_estimate=pl.CostEstimate(flops=0, bytes_accessed=4_000_000, transcendentals=0),
        name="place_tiles",
    )(details, tiles, place)


def tiles_kernel(parts, segments, chips, groups, blocks, relations, *refs):
    place_ref, refs = refs[0], refs[1:]
    buffers, refs = refs[: len(segments)], refs[len(segments) :]
    payloads, refs = refs[: len(parts)], refs[len(parts) :]
    near_ref, far_ref, grad_far, grad_own, summed = refs[:5]
    adjoint, total, vector, codes, sem, landed = refs[5:]
    chip, group, core = place_ref[0], place_ref[1], place_ref[2]
    piece = adjoint.shape[1] // groups
    moves = {j: [] for j in range(chips)}
    for buffer, (level, origins) in zip(buffers, segments, strict=True):
        for q, origin in enumerate(origins):
            start = jnp.where(core == 0, origin[0], origin[1]) ^ group
            start = pl.multiple_of(start * piece, piece)
            for n, j in enumerate(level):
                moves[j].append(
                    pltpu.make_async_copy(
                        buffer.at[pl.ds((q * len(level) + n) * piece, piece)],
                        adjoint.at[j, pl.ds(start, piece)],
                        landed.at[j, len(moves[j])],
                    )
                )
    for j in range(chips):
        for move in moves[j]:
            move.start()
    edge = payloads[0].shape[-1]
    copies = {}
    for payload, (j, first, size) in zip(payloads, parts, strict=True):
        if first == 0:
            vector[j] = payload[size * edge :, :].astype(jnp.float32).astype(jnp.int32)
            copies[j] = pltpu.make_async_copy(vector.at[j], codes.at[j], sem.at[j])
            copies[j].start()
    total[...] = jnp.zeros_like(total)

    def add(j, payload, slot, p):
        row = pl.multiple_of(codes[j, slot + p, 1] * edge, edge)
        partial = lax.dot_general(
            payload[pl.ds(pl.multiple_of(p * edge, edge), edge), :],
            adjoint[j, pl.ds(row, edge), :],
            (((0,), (0,)), ((), ())),
            preferred_element_type=jnp.float32,
        )
        total[codes[j, slot + p, 0]] += partial.astype(jnp.bfloat16).astype(jnp.float32)

    for payload, (j, first, size) in zip(payloads, parts, strict=True):
        if first == 0:
            copies[j].wait()
            for move in moves[j]:
                move.wait()
        unroll = next(u for u in range(min(size, 8), 0, -1) if size % u == 0)
        if unroll == 1:
            unroll = size

        def some(i, carry):
            for u in range(unroll):
                add(j, payload, first, i * unroll + u)
            return carry

        lax.fori_loop(0, size // unroll, some, 0)

    rows = blocks * edge
    share = near_ref.shape[0] // (chips * CORES)
    for r in range(relations):
        for h in range(CORES):
            part = total[pl.ds((h * relations + r) * blocks, blocks)].astype(jnp.bfloat16)
            summed[h, r] = part.reshape(rows, part.shape[-1])
        grad = jnp.dot(near_ref[...], summed[core, r], preferred_element_type=jnp.float32)
        grad += jnp.dot(far_ref[...], summed[1 - core, r], preferred_element_type=jnp.float32)
        for far in range(CORES):
            out = grad_far if far else grad_own
            for c in range(chips):
                for h in range(CORES):
                    slab = grad[(c * CORES + h) * share : (c * CORES + h + 1) * share]

                    @pl.when(h == (core ^ far))
                    def _():
                        out[chip ^ c, r] = slab.astype(out.dtype)


def tiles_and_grad(parts, segments, place, buffers, payloads, near, far, sizes):
    chips, groups, blocks, relations = sizes
    feature, rows = near.shape
    edge = rows // blocks
    shape = (chips, relations, feature // (chips * CORES), feature)
    return pl.pallas_call(
        functools.partial(tiles_kernel, parts, segments, chips, groups, blocks, relations),
        out_shape=[
            jax.ShapeDtypeStruct(shape, jnp.bfloat16),
            jax.ShapeDtypeStruct(shape, jnp.float32),
            jax.ShapeDtypeStruct((CORES, relations, rows, feature), jnp.bfloat16),
        ],
        in_specs=[SMEM] + [ANY] * len(buffers) + [VMEM] * (2 + len(payloads)),
        out_specs=[VMEM] * 3,
        scratch_shapes=[
            pltpu.VMEM((chips, rows, feature), jnp.bfloat16),
            pltpu.VMEM((CORES * relations * blocks, edge, feature), jnp.float32),
            pltpu.VMEM((chips, SLOTS, edge), jnp.int32),
            pltpu.SMEM((chips, SLOTS, edge), jnp.int32),
            pltpu.SemaphoreType.DMA((chips,)),
            pltpu.SemaphoreType.DMA((chips, groups)),
        ],
        compiler_params=pltpu.CompilerParams(vmem_limit_bytes=LIMIT),
        cost_estimate=pl.CostEstimate(flops=0, bytes_accessed=1_000_000, transcendentals=0),
        name="tiles_and_grad",
    )(place, *buffers, *payloads, near, far)


def rows_kernel(groups, relations, far, place_ref, summed, weights_ref, out):
    group, core = place_ref[1], place_ref[2]
    piece = summed.shape[2] // groups
    value = None
    for r in range(relations):
        term = lax.dot_general(
            summed[core ^ far, r],
            weights_ref[r],
            (((1,), (1,)), ((), ())),
            preferred_element_type=jnp.float32,
        )
        value = term if value is None else value + term
    for q in range(groups):
        out[group ^ q] = value[q * piece : (q + 1) * piece].astype(out.dtype)


def row_terms(place, summed, weights, groups, far, dtype):
    _, relations, rows, feature = summed.shape
    return pl.pallas_call(
        functools.partial(rows_kernel, groups, relations, far),
        out_shape=jax.ShapeDtypeStruct((groups, rows // groups, feature), dtype),
        in_specs=[SMEM, VMEM, VMEM],
        out_specs=VMEM,
        compiler_params=pltpu.CompilerParams(vmem_limit_bytes=LIMIT),
        cost_estimate=pl.CostEstimate(
            flops=4 * rows * feature * feature, bytes_accessed=4_000_000, transcendentals=0
        ),
        name="row_terms",
    )(place, summed, weights)


def plane_masks(groups, core):
    masks = [1 << i for i in range(groups.bit_length() - 1)]
    return masks[::-1] if core % CORES else masks


def after(value, *others):
    return lax.optimization_barrier((value, *others))[0]


def on_device(
    out_adjoint,
    layer_input,
    rel_weights,
    self_weight,
    tile_values,
    tile_rel,
    tile_target,
    tile_src,
    tile_dest,
):
    nodes = lax.axis_size("node")
    groups = lax.axis_size("rel")
    chips = nodes // CORES
    node = lax.axis_index("node")
    group = lax.axis_index("rel")
    chip, core = node // CORES, node % CORES
    edge = tile_values.shape[-1]
    rows = layer_input.shape[1]
    blocks = rows // edge
    relations = rel_weights.shape[0]

    def across(value, axis, size, mask):
        return lax.ppermute(value, axis, [(i, i ^ mask) for i in range(size)])

    def to_chip(value, j):
        return across(value, "node", nodes, CORES * j)

    def in_plane(value, step):
        pairs = []
        for g in range(groups):
            for n in range(nodes):
                mask = plane_masks(groups, n)[step]
                pairs.append((g * nodes + n, (g ^ mask) * nodes + n))
        return lax.ppermute(value, ("rel", "node"), pairs)

    own = out_adjoint[0]
    place = jnp.stack([chip, group, core]).astype(jnp.int32)
    details = jnp.stack([tile_dest[0, :, 0], tile_rel[0], tile_target[0], tile_src[0]])

    levels = [
        [j for j in range(chips) if j.bit_count() == count]
        for count in range(chips.bit_length())
    ]
    levels[:2] = [levels[0] + levels[1]]
    steps = groups.bit_length() - 1
    near = layer_input[0].T
    far = across(near, "node", nodes, 1)
    mid = chips // 2
    parts = [(0, 0, SLOTS), (mid, 0, HEAD), (mid, HEAD, SLOTS - HEAD)]
    parts = tuple(parts + [(j, 0, SLOTS) for j in range(chips - 1, 0, -1) if j != mid])
    placed = place_tiles(parts, chips, blocks, relations, details, tile_values[0], place)

    by_chip = {0: own}
    for j in levels[0][1:]:
        by_chip[j] = to_chip(own, j)
    head = to_chip(placed[1], mid)
    first = [head, far] + [by_chip[j] for j in levels[0][1:]]
    body = to_chip(after(placed[2], *first), mid)
    payloads = [placed[0], head, body]
    for value, (j, _, _) in list(zip(placed, parts, strict=True))[3:]:
        payloads.append(to_chip(after(value, *first, *([body] if j == 1 else [])), j))
    for level in levels[1:]:
        for j in level:
            bit = j & -j
            by_chip[j] = to_chip(after(by_chip[j ^ bit], *first), bit)

    buffers, segments = [], []
    for n, level in enumerate(levels):
        held = [by_chip[j] for j in level]
        held = held[0] if len(held) == 1 else jnp.concatenate(held)
        if n == 0:
            held = after(held, *first)
        held = [(held, ((0, 0),))]
        for step in range(steps):
            if n:
                merged = jnp.concatenate([value for value, _ in held]) if step else held[0][0]
                held = [(merged, sum((origins for _, origins in held), ()))]
            masks = [plane_masks(groups, c)[step] for c in range(CORES)]
            held = held + [
                (in_plane(value, step), tuple((a ^ masks[0], b ^ masks[1]) for a, b in origins))
                for value, origins in held
            ]
        for value, origins in held:
            buffers.append(value)
            segments.append((level, origins))
    sizes = (chips, groups, blocks, relations)
    grad_far, grad_own, summed = tiles_and_grad(
        parts, segments, place, buffers, payloads, near, far, sizes
    )
    grad_far = across(grad_far, "node", nodes, 1)
    rows_far = row_terms(place, summed, rel_weights, groups, 1, jnp.bfloat16)
    rows_far = across(rows_far, "node", nodes, 1)
    rows_own = row_terms(place, summed, rel_weights, groups, 0, jnp.float32)
    grad = grad_own + grad_far.astype(jnp.float32)
    others = [to_chip(grad[j].astype(jnp.bfloat16), j) for j in range(1, chips)]
    rel_weight_grad = grad[0]
    for other in others:
        rel_weight_grad += other.astype(jnp.float32)

    totals = rows_own + rows_far.astype(jnp.float32)
    others = [
        across(totals[m].astype(jnp.bfloat16), "rel", groups, m) for m in range(1, groups)
    ]
    d_source = totals[0] + jnp.einsum(
        "vj,ij->vi", own, self_weight, preferred_element_type=jnp.float32
    )
    for other in others:
        d_source += other.astype(jnp.float32)
    return rel_weight_grad, d_source.astype(jnp.bfloat16)[None]


def solution(mesh):
    return jax.shard_map(
        on_device,
        mesh=mesh,
        in_specs=(
            P("node", "rel", None),
            P("node", None, None),
            P("rel", None, None),
            P(),
            P("rel", "node", None, None),
            P("rel", "node"),
            P("rel", "node"),
            P("rel", "node"),
            P("rel", "node", None),
        ),
        out_specs=(P("rel", "node", None), P("node", "rel", None)),
        check_vma=False,
    )
```

```python
import functools

import jax
import jax.numpy as jnp
from jax import lax
from jax.experimental import pallas as pl
from jax.experimental.pallas import tpu as pltpu
from jax.sharding import PartitionSpec as P

CAPACITY = 8
CORES = 2
SLOTS = CORES * CAPACITY
LIMIT = 24 * 1024 * 1024
HEAD = 5
SMEM = pl.BlockSpec(memory_space=pltpu.SMEM)
VMEM = pl.BlockSpec(memory_space=pltpu.VMEM)
ANY = pl.BlockSpec(memory_space=pl.ANY)


def payload_rows(edge, first, size):
    return size * edge + (SLOTS if first == 0 else 0)


def place_kernel(parts, chips, blocks, relations, *refs):
    given, place_ref, outs = refs[:2], refs[2], refs[3 : 3 + len(parts)]
    details, tiles_ref, order, count, sem = refs[3 + len(parts) :]
    copies = [
        pltpu.make_async_copy(given[0], details, sem.at[0]),
        pltpu.make_async_copy(given[1], tiles_ref, sem.at[1]),
    ]
    for copy in copies:
        copy.start()
    chip = place_ref[0]
    edge = tiles_ref.shape[-1]
    for j in range(chips):
        count[j] = 0
    for s in range(chips * SLOTS):
        order[s] = 0
    copies[0].wait()

    def rank(t, carry):
        j = (details[0, t] // CORES) ^ chip
        p = count[j]
        order[j * SLOTS + p] = t
        count[j] = p + 1
        return carry

    lax.fori_loop(0, details.shape[1], rank, 0)
    copies[1].wait()
    lane = lax.broadcasted_iota(jnp.int32, (SLOTS, edge), 1)
    row = lax.broadcasted_iota(jnp.int32, (SLOTS, edge), 0)
    for out, (j, first, size) in zip(outs, parts, strict=True):
        for p in range(size):
            tile = tiles_ref[order[j * SLOTS + first + p]]
            full = first + p < count[j]
            out[p * edge : (p + 1) * edge, :] = jnp.where(full, tile, jnp.zeros_like(tile))
        if first == 0:
            codes = jnp.zeros((SLOTS, edge), jnp.int32)
            for p in range(SLOTS):
                t = order[j * SLOTS + p]
                bucket = (details[0, t] % CORES) * relations + details[1, t]
                code = jnp.where(lane == 0, bucket * blocks + details[3, t], details[2, t])
                codes = jnp.where(row == p, code, codes)
            out[size * edge :, :] = codes.astype(jnp.float32).astype(jnp.bfloat16)


def place_tiles(parts, chips, blocks, relations, details, tiles, place):
    edge = tiles.shape[-1]
    shapes = [
        jax.ShapeDtypeStruct((payload_rows(edge, first, size), edge), tiles.dtype)
        for _, first, size in parts
    ]
    return pl.pallas_call(
        functools.partial(place_kernel, parts, chips, blocks, relations),
        out_shape=shapes,
        in_specs=[ANY] * 2 + [SMEM],
        out_specs=[VMEM] * len(shapes),
        scratch_shapes=[
            pltpu.SMEM(details.shape, jnp.int32),
            pltpu.VMEM(tiles.shape, tiles.dtype),
            pltpu.SMEM((chips * SLOTS,), jnp.int32),
            pltpu.SMEM((chips,), jnp.int32),
            pltpu.SemaphoreType.DMA((2,)),
        ],
        compiler_params=pltpu.CompilerParams(vmem_limit_bytes=LIMIT),
        cost_estimate=pl.CostEstimate(flops=0, bytes_accessed=4_000_000, transcendentals=0),
        name="place_tiles",
    )(details, tiles, place)


def read_codes(parts, payloads, vector, codes, sem):
    copies = {}
    for payload, (j, first, size) in zip(payloads, parts, strict=True):
        if first == 0:
            last = payload[payload.shape[0] - SLOTS :, :]
            vector[j] = last.astype(jnp.float32).astype(jnp.int32)
            copies[j] = pltpu.make_async_copy(vector.at[j], codes.at[j], sem.at[j])
            copies[j].start()
    return copies


def gather_moves(buffers, segments, place_ref, groups, adjoint, landed):
    group, core = place_ref[1], place_ref[2]
    piece = adjoint.shape[1] // groups
    where = sorted({j for level, _ in segments for j in level})
    moves = {j: [] for j in where}
    for buffer, (level, origins) in zip(buffers, segments, strict=True):
        for q, origin in enumerate(origins):
            start = jnp.where(core == 0, origin[0], origin[1]) ^ group
            start = pl.multiple_of(start * piece, piece)
            for n, j in enumerate(level):
                moves[j].append(
                    pltpu.make_async_copy(
                        buffer.at[pl.ds((q * len(level) + n) * piece, piece)],
                        adjoint.at[where.index(j), pl.ds(start, piece)],
                        landed.at[where.index(j), len(moves[j])],
                    )
                )
                moves[j][-1].start()
    return where, moves


def add_tiles(payload, j, first, size, adjoint, total, codes):
    edge = payload.shape[-1]
    unroll = next(u for u in range(min(size, 8), 0, -1) if size % u == 0)
    if unroll == 1:
        unroll = size

    def some(i, carry):
        for u in range(unroll):
            p = i * unroll + u
            row = pl.multiple_of(codes[j, first + p, 1] * edge, edge)
            partial = lax.dot_general(
                payload[pl.ds(pl.multiple_of(p * edge, edge), edge), :],
                adjoint[pl.ds(row, edge), :],
                (((0,), (0,)), ((), ())),
                preferred_element_type=jnp.float32,
            )
            total[codes[j, first + p, 0]] += partial.astype(jnp.bfloat16).astype(jnp.float32)
        return carry

    lax.fori_loop(0, size // unroll, some, 0)


def early_kernel(parts, segments, groups, place_ref, *refs):
    buffers, refs = refs[: len(segments)], refs[len(segments) :]
    payloads, refs = refs[: len(parts)], refs[len(parts) :]
    adjoint, total, vector, codes, sem, landed = refs
    where, moves = gather_moves(buffers, segments, place_ref, groups, adjoint, landed)
    copies = read_codes(parts, payloads, vector, codes, sem)
    total[...] = jnp.zeros_like(total)
    for j in where:
        for move in moves[j]:
            move.wait()
    for payload, (j, first, size) in zip(payloads, parts, strict=True):
        if first == 0:
            copies[j].wait()
        add_tiles(payload, j, first, size, adjoint.at[where.index(j)], total, codes)


def early_tiles(parts, segments, place, buffers, payloads, sizes):
    chips, groups, blocks, relations = sizes
    edge, feature = payloads[0].shape[-1], buffers[0].shape[-1]
    held = len({j for level, _ in segments for j in level})
    return pl.pallas_call(
        functools.partial(early_kernel, parts, segments, groups),
        out_shape=[
            jax.ShapeDtypeStruct((held, blocks * edge, feature), jnp.bfloat16),
            jax.ShapeDtypeStruct((CORES * relations * blocks, edge, feature), jnp.float32),
        ],
        in_specs=[SMEM] + [ANY] * len(buffers) + [VMEM] * len(payloads),
        out_specs=[VMEM] * 2,
        scratch_shapes=[
            pltpu.VMEM((chips, SLOTS, edge), jnp.int32),
            pltpu.SMEM((chips, SLOTS, edge), jnp.int32),
            pltpu.SemaphoreType.DMA((chips,)),
            pltpu.SemaphoreType.DMA((held, groups)),
        ],
        compiler_params=pltpu.CompilerParams(vmem_limit_bytes=LIMIT),
        cost_estimate=pl.CostEstimate(flops=0, bytes_accessed=1_000_000, transcendentals=0),
        name="early_tiles",
    )(place, *buffers, *payloads)


def late_kernel(parts, held, segments, sizes, place_ref, adjoint, before, *refs):
    chips, groups, blocks, relations = sizes
    buffers, refs = refs[: len(segments)], refs[len(segments) :]
    payloads, refs = refs[: len(parts)], refs[len(parts) :]
    near_ref, far_ref, grad_far, grad_own, summed, total = refs[:6]
    late, vector, codes, sem, landed = refs[6:]
    chip, core = place_ref[0], place_ref[2]
    edge = payloads[0].shape[-1]
    where, moves = gather_moves(buffers, segments, place_ref, groups, late, landed)
    copies = read_codes(parts, payloads, vector, codes, sem)
    for payload, (j, first, size) in zip(payloads, parts, strict=True):
        if first == 0:
            copies[j].wait()
            for move in moves.get(j, []):
                move.wait()
        shard = late.at[where.index(j)] if j in where else adjoint.at[held.index(j)]
        add_tiles(payload, j, first, size, shard, total, codes)

    rows = blocks * edge
    share = near_ref.shape[0] // (chips * CORES)
    for r in range(relations):
        for h in range(CORES):
            part = total[pl.ds((h * relations + r) * blocks, blocks)].astype(jnp.bfloat16)
            summed[h, r] = part.reshape(rows, part.shape[-1])
        grad = jnp.dot(near_ref[...], summed[core, r], preferred_element_type=jnp.float32)
        grad += jnp.dot(far_ref[...], summed[1 - core, r], preferred_element_type=jnp.float32)
        for far in range(CORES):
            out = grad_far if far else grad_own
            for c in range(chips):
                for h in range(CORES):
                    slab = grad[(c * CORES + h) * share : (c * CORES + h + 1) * share]

                    @pl.when(h == (core ^ far))
                    def _():
                        out[chip ^ c, r] = slab.astype(out.dtype)


def late_tiles_and_grad(parts, held, segments, place, adjoint, total, buffers, payloads, inputs, sizes):
    chips, groups, blocks, relations = sizes
    feature, rows = inputs[0].shape
    edge = rows // blocks
    shape = (chips, relations, feature // (chips * CORES), feature)
    behind = len({j for level, _ in segments for j in level})
    return pl.pallas_call(
        functools.partial(late_kernel, parts, held, segments, sizes),
        out_shape=[
            jax.ShapeDtypeStruct(shape, jnp.bfloat16),
            jax.ShapeDtypeStruct(shape, jnp.float32),
            jax.ShapeDtypeStruct((CORES, relations, rows, feature), jnp.bfloat16),
            jax.ShapeDtypeStruct(total.shape, total.dtype),
        ],
        in_specs=[SMEM] + [VMEM] * 2 + [ANY] * len(buffers) + [VMEM] * (2 + len(payloads)),
        out_specs=[VMEM] * 4,
        scratch_shapes=[
            pltpu.VMEM((behind, rows, feature), jnp.bfloat16),
            pltpu.VMEM((chips, SLOTS, edge), jnp.int32),
            pltpu.SMEM((chips, SLOTS, edge), jnp.int32),
            pltpu.SemaphoreType.DMA((chips,)),
            pltpu.SemaphoreType.DMA((behind, groups)),
        ],
        input_output_aliases={2: 3},
        compiler_params=pltpu.CompilerParams(vmem_limit_bytes=LIMIT),
        cost_estimate=pl.CostEstimate(flops=0, bytes_accessed=1_000_000, transcendentals=0),
        name="late_tiles_and_grad",
    )(place, adjoint, total, *buffers, *payloads, *inputs)


def turn_kernel(*refs):
    half = len(refs) // 2
    for source, target in zip(refs[:half], refs[half:], strict=True):
        target[...] = source[...].T


def turned(*arrays):
    return pl.pallas_call(
        turn_kernel,
        out_shape=[jax.ShapeDtypeStruct(a.shape[::-1], a.dtype) for a in arrays],
        in_specs=[VMEM] * len(arrays),
        out_specs=[VMEM] * len(arrays),
        compiler_params=pltpu.CompilerParams(vmem_limit_bytes=LIMIT),
        cost_estimate=pl.CostEstimate(flops=0, bytes_accessed=1_000_000, transcendentals=0),
        name="turn_inputs",
    )(*arrays)


def rows_kernel(groups, relations, far, place_ref, summed, weights_ref, out):
    group, core = place_ref[1], place_ref[2]
    piece = summed.shape[2] // groups
    value = None
    for r in range(relations):
        term = lax.dot_general(
            summed[core ^ far, r],
            weights_ref[r],
            (((1,), (1,)), ((), ())),
            preferred_element_type=jnp.float32,
        )
        value = term if value is None else value + term
    for q in range(groups):
        out[group ^ q] = value[q * piece : (q + 1) * piece].astype(out.dtype)


def row_terms(place, summed, weights, groups, far, dtype):
    _, relations, rows, feature = summed.shape
    return pl.pallas_call(
        functools.partial(rows_kernel, groups, relations, far),
        out_shape=jax.ShapeDtypeStruct((groups, rows // groups, feature), dtype),
        in_specs=[SMEM, VMEM, VMEM],
        out_specs=VMEM,
        compiler_params=pltpu.CompilerParams(vmem_limit_bytes=LIMIT),
        cost_estimate=pl.CostEstimate(
            flops=4 * rows * feature * feature, bytes_accessed=4_000_000, transcendentals=0
        ),
        name="row_terms",
    )(place, summed, weights)


def plane_masks(groups, core):
    masks = [1 << i for i in range(groups.bit_length() - 1)]
    return masks[::-1] if core % CORES else masks


def after(value, *others):
    return lax.optimization_barrier((value, *others))[0]


def on_device(
    out_adjoint,
    layer_input,
    rel_weights,
    self_weight,
    tile_values,
    tile_rel,
    tile_target,
    tile_src,
    tile_dest,
):
    nodes = lax.axis_size("node")
    groups = lax.axis_size("rel")
    chips = nodes // CORES
    node = lax.axis_index("node")
    group = lax.axis_index("rel")
    chip, core = node // CORES, node % CORES
    edge = tile_values.shape[-1]
    rows = layer_input.shape[1]
    blocks = rows // edge
    relations = rel_weights.shape[0]

    def across(value, axis, size, mask):
        return lax.ppermute(value, axis, [(i, i ^ mask) for i in range(size)])

    def to_chip(value, j):
        return across(value, "node", nodes, CORES * j)

    def in_plane(value, step):
        pairs = []
        for g in range(groups):
            for n in range(nodes):
                mask = plane_masks(groups, n)[step]
                pairs.append((g * nodes + n, (g ^ mask) * nodes + n))
        return lax.ppermute(value, ("rel", "node"), pairs)

    own = out_adjoint[0]
    place = jnp.stack([chip, group, core]).astype(jnp.int32)
    details = jnp.stack([tile_dest[0, :, 0], tile_rel[0], tile_target[0], tile_src[0]])

    levels = [
        [j for j in range(chips) if j.bit_count() == count]
        for count in range(chips.bit_length())
    ]
    levels[:2] = [levels[0] + levels[1]]
    steps = groups.bit_length() - 1
    near = layer_input[0]
    far = across(near, "node", nodes, 1)
    mid = chips // 2
    parts = [(0, 0, SLOTS), (mid, 0, HEAD), (mid, HEAD, SLOTS - HEAD)]
    parts = tuple(parts + [(j, 0, SLOTS) for j in range(chips - 1, 0, -1) if j != mid])
    placed = place_tiles(parts, chips, blocks, relations, details, tile_values[0], place)

    by_chip = {0: own}
    for j in levels[0][1:]:
        by_chip[j] = to_chip(own, j)
    head = to_chip(placed[1], mid)
    first = [head, far] + [by_chip[j] for j in levels[0][1:]]
    body = to_chip(after(placed[2], *first), mid)
    payloads = [placed[0], head, body]
    for value, (j, _, _) in list(zip(placed, parts, strict=True))[3:]:
        payloads.append(to_chip(after(value, *first, *([body] if j == 1 else [])), j))
    for level in levels[1:]:
        for j in level:
            bit = j & -j
            by_chip[j] = to_chip(after(by_chip[j ^ bit], *first), bit)

    buffers, segments = [], []
    for n, level in enumerate(levels):
        held = [by_chip[j] for j in level]
        held = held[0] if len(held) == 1 else jnp.concatenate(held)
        if n == 0:
            held = after(held, *first)
        held = [(held, ((0, 0),))]
        for step in range(steps):
            if n:
                merged = jnp.concatenate([value for value, _ in held]) if step else held[0][0]
                held = [(merged, sum((origins for _, origins in held), ()))]
            masks = [plane_masks(groups, c)[step] for c in range(CORES)]
            held = held + [
                (in_plane(value, step), tuple((a ^ masks[0], b ^ masks[1]) for a, b in origins))
                for value, origins in held
            ]
        for value, origins in held:
            buffers.append(value)
            segments.append((level, origins))
    near, far = turned(near, far)
    sizes = (chips, groups, blocks, relations)
    early = [i for i, (j, _, _) in enumerate(parts) if j in (0, mid)]
    late = [i for i in range(len(parts)) if i not in early][::-1]
    split = sum(level == levels[0] for level, _ in segments)
    adjoint, total = early_tiles(
        tuple(parts[i] for i in early),
        segments[:split],
        place,
        buffers[:split],
        [payloads[i] for i in early],
        sizes,
    )
    grad_far, grad_own, summed, _ = late_tiles_and_grad(
        tuple(parts[i] for i in late),
        sorted(levels[0]),
        segments[split:],
        place,
        adjoint,
        total,
        buffers[split:],
        [payloads[i] for i in late],
        [near, far],
        sizes,
    )
    grad_far = across(grad_far, "node", nodes, 1)
    rows_far = row_terms(place, summed, rel_weights, groups, 1, jnp.bfloat16)
    rows_far = across(rows_far, "node", nodes, 1)
    rows_own = row_terms(place, summed, rel_weights, groups, 0, jnp.float32)
    grad = grad_own + grad_far.astype(jnp.float32)
    others = [to_chip(grad[j].astype(jnp.bfloat16), j) for j in range(1, chips)]
    rel_weight_grad = grad[0]
    for other in others:
        rel_weight_grad += other.astype(jnp.float32)

    totals = rows_own + rows_far.astype(jnp.float32)
    others = [
        across(totals[m].astype(jnp.bfloat16), "rel", groups, m) for m in range(1, groups)
    ]
    d_source = totals[0] + jnp.einsum(
        "vj,ij->vi", own, self_weight, preferred_element_type=jnp.float32
    )
    for other in others:
        d_source += other.astype(jnp.float32)
    return rel_weight_grad, d_source.astype(jnp.bfloat16)[None]


def solution(mesh):
    return jax.shard_map(
        on_device,
        mesh=mesh,
        in_specs=(
            P("node", "rel", None),
            P("node", None, None),
            P("rel", None, None),
            P(),
            P("rel", "node", None, None),
            P("rel", "node"),
            P("rel", "node"),
            P("rel", "node"),
            P("rel", "node", None),
        ),
        out_specs=(P("rel", "node", None), P("node", "rel", None)),
        check_vma=False,
    )
```

```python
import functools

import jax
import jax.numpy as jnp
from jax import lax
from jax.experimental import pallas as pl
from jax.experimental.pallas import tpu as pltpu
from jax.sharding import PartitionSpec as P

CAPACITY = 8
CORES = 2
SLOTS = CORES * CAPACITY
LIMIT = 24 * 1024 * 1024
HEAD = 3
SMEM = pl.BlockSpec(memory_space=pltpu.SMEM)
VMEM = pl.BlockSpec(memory_space=pltpu.VMEM)
ANY = pl.BlockSpec(memory_space=pl.ANY)


def payload_rows(edge, first, size):
    return size * edge + (SLOTS if first == 0 else 0)


def place_kernel(parts, chips, blocks, relations, *refs):
    given, place_ref, outs = refs[:2], refs[2], refs[3 : 3 + len(parts)]
    details, tiles_ref, order, count, sem = refs[3 + len(parts) :]
    copies = [
        pltpu.make_async_copy(given[0], details, sem.at[0]),
        pltpu.make_async_copy(given[1], tiles_ref, sem.at[1]),
    ]
    for copy in copies:
        copy.start()
    chip = place_ref[0]
    edge = tiles_ref.shape[-1]
    for j in range(chips):
        count[j] = 0
    for s in range(chips * SLOTS):
        order[s] = 0
    copies[0].wait()

    def rank(t, carry):
        j = (details[0, t] // CORES) ^ chip
        p = count[j]
        order[j * SLOTS + p] = t
        count[j] = p + 1
        return carry

    lax.fori_loop(0, details.shape[1], rank, 0)
    copies[1].wait()
    lane = lax.broadcasted_iota(jnp.int32, (SLOTS, edge), 1)
    row = lax.broadcasted_iota(jnp.int32, (SLOTS, edge), 0)
    for out, (j, first, size) in zip(outs, parts, strict=True):
        for p in range(size):
            tile = tiles_ref[order[j * SLOTS + first + p]]
            full = first + p < count[j]
            out[p * edge : (p + 1) * edge, :] = jnp.where(full, tile, jnp.zeros_like(tile))
        if first == 0:
            codes = jnp.zeros((SLOTS, edge), jnp.int32)
            for p in range(SLOTS):
                t = order[j * SLOTS + p]
                bucket = (details[0, t] % CORES) * relations + details[1, t]
                code = jnp.where(lane == 0, bucket * blocks + details[3, t], details[2, t])
                codes = jnp.where(row == p, code, codes)
            out[size * edge :, :] = codes.astype(jnp.float32).astype(jnp.bfloat16)


def place_tiles(parts, chips, blocks, relations, details, tiles, place):
    edge = tiles.shape[-1]
    shapes = [
        jax.ShapeDtypeStruct((payload_rows(edge, first, size), edge), tiles.dtype)
        for _, first, size in parts
    ]
    return pl.pallas_call(
        functools.partial(place_kernel, parts, chips, blocks, relations),
        out_shape=shapes,
        in_specs=[ANY] * 2 + [SMEM],
        out_specs=[VMEM] * len(shapes),
        scratch_shapes=[
            pltpu.SMEM(details.shape, jnp.int32),
            pltpu.VMEM(tiles.shape, tiles.dtype),
            pltpu.SMEM((chips * SLOTS,), jnp.int32),
            pltpu.SMEM((chips,), jnp.int32),
            pltpu.SemaphoreType.DMA((2,)),
        ],
        compiler_params=pltpu.CompilerParams(vmem_limit_bytes=LIMIT),
        cost_estimate=pl.CostEstimate(flops=0, bytes_accessed=4_000_000, transcendentals=0),
        name="place_tiles",
    )(details, tiles, place)


def read_codes(parts, payloads, vector, codes, sem):
    copies = {}
    for payload, (j, first, size) in zip(payloads, parts, strict=True):
        if first == 0:
            last = payload[payload.shape[0] - SLOTS :, :]
            vector[j] = last.astype(jnp.float32).astype(jnp.int32)
            copies[j] = pltpu.make_async_copy(vector.at[j], codes.at[j], sem.at[j])
            copies[j].start()
    return copies


def gather_moves(buffers, segments, place_ref, groups, adjoint, landed):
    group, core = place_ref[1], place_ref[2]
    piece = adjoint.shape[1] // groups
    where = sorted({j for level, _ in segments for j in level})
    moves = {j: [] for j in where}
    for buffer, (level, origins) in zip(buffers, segments, strict=True):
        for q, origin in enumerate(origins):
            start = jnp.where(core == 0, origin[0], origin[1]) ^ group
            start = pl.multiple_of(start * piece, piece)
            for n, j in enumerate(level):
                moves[j].append(
                    pltpu.make_async_copy(
                        buffer.at[pl.ds((q * len(level) + n) * piece, piece)],
                        adjoint.at[where.index(j), pl.ds(start, piece)],
                        landed.at[where.index(j), len(moves[j])],
                    )
                )
                moves[j][-1].start()
    return where, moves


def add_tiles(payload, j, first, size, adjoint, total, codes):
    edge = payload.shape[-1]
    unroll = next(u for u in range(min(size, 8), 0, -1) if size % u == 0)
    if unroll == 1:
        unroll = size

    def some(i, carry):
        for u in range(unroll):
            p = i * unroll + u
            row = pl.multiple_of(codes[j, first + p, 1] * edge, edge)
            partial = lax.dot_general(
                payload[pl.ds(pl.multiple_of(p * edge, edge), edge), :],
                adjoint[pl.ds(row, edge), :],
                (((0,), (0,)), ((), ())),
                preferred_element_type=jnp.float32,
            )
            total[codes[j, first + p, 0]] += partial.astype(jnp.bfloat16).astype(jnp.float32)
        return carry

    lax.fori_loop(0, size // unroll, some, 0)


def early_kernel(parts, segments, groups, place_ref, *refs):
    buffers, refs = refs[: len(segments)], refs[len(segments) :]
    payloads, refs = refs[: len(parts)], refs[len(parts) :]
    adjoint, total, vector, codes, sem, landed = refs
    where, moves = gather_moves(buffers, segments, place_ref, groups, adjoint, landed)
    copies = read_codes(parts, payloads, vector, codes, sem)
    total[...] = jnp.zeros_like(total)
    for j in where:
        for move in moves[j]:
            move.wait()
    for payload, (j, first, size) in zip(payloads, parts, strict=True):
        if first == 0:
            copies[j].wait()
        add_tiles(payload, j, first, size, adjoint.at[where.index(j)], total, codes)


def early_tiles(parts, segments, place, buffers, payloads, sizes):
    chips, groups, blocks, relations = sizes
    edge, feature = payloads[0].shape[-1], buffers[0].shape[-1]
    held = len({j for level, _ in segments for j in level})
    return pl.pallas_call(
        functools.partial(early_kernel, parts, segments, groups),
        out_shape=[
            jax.ShapeDtypeStruct((held, blocks * edge, feature), jnp.bfloat16),
            jax.ShapeDtypeStruct((CORES * relations * blocks, edge, feature), jnp.float32),
        ],
        in_specs=[SMEM] + [ANY] * len(buffers) + [VMEM] * len(payloads),
        out_specs=[VMEM] * 2,
        scratch_shapes=[
            pltpu.VMEM((chips, SLOTS, edge), jnp.int32),
            pltpu.SMEM((chips, SLOTS, edge), jnp.int32),
            pltpu.SemaphoreType.DMA((chips,)),
            pltpu.SemaphoreType.DMA((held, groups)),
        ],
        compiler_params=pltpu.CompilerParams(vmem_limit_bytes=LIMIT),
        cost_estimate=pl.CostEstimate(flops=0, bytes_accessed=1_000_000, transcendentals=0),
        name="early_tiles",
    )(place, *buffers, *payloads)


def late_kernel(parts, held, segments, sizes, place_ref, adjoint, before, *refs):
    chips, groups, blocks, relations = sizes
    buffers, refs = refs[: len(segments)], refs[len(segments) :]
    payloads, refs = refs[: len(parts)], refs[len(parts) :]
    weights_ref, rows_far, summed, total, late, vector, codes, sem, landed = refs
    edge = payloads[0].shape[-1]
    where, moves = gather_moves(buffers, segments, place_ref, groups, late, landed)
    copies = read_codes(parts, payloads, vector, codes, sem)
    for payload, (j, first, size) in zip(payloads, parts, strict=True):
        if first == 0:
            copies[j].wait()
            for move in moves.get(j, []):
                move.wait()
        shard = late.at[where.index(j)] if j in where else adjoint.at[held.index(j)]
        add_tiles(payload, j, first, size, shard, total, codes)

    for h in range(CORES):
        for r in range(relations):
            part = total[pl.ds((h * relations + r) * blocks, blocks)].astype(jnp.bfloat16)
            summed[h, r] = part.reshape(blocks * edge, part.shape[-1])
    for spot, value in multiply_rows(place_ref, summed, weights_ref, groups, 1):
        rows_far[spot] = value.astype(rows_far.dtype)


def multiply_rows(place_ref, summed, weights_ref, groups, far):
    group, core = place_ref[1], place_ref[2]
    piece = summed.shape[2] // groups
    steps = groups.bit_length() - 1
    value = None
    for r in range(summed.shape[1]):
        term = lax.dot_general(
            summed[core ^ far, r],
            weights_ref[r],
            (((1,), (1,)), ((), ())),
            preferred_element_type=jnp.float32,
        )
        value = term if value is None else value + term
    pieces = []
    for q in range(groups):
        mask = group ^ q
        spot = [0, 0]
        for step in range(steps):
            for c in range(CORES):
                bit = plane_masks(groups, c)[step].bit_length() - 1
                spot[c] = spot[c] + (((mask >> bit) & 1) << (steps - 1 - step))
        spot = jnp.where((core ^ far) == 0, spot[0], spot[1])
        pieces.append((spot, value[q * piece : (q + 1) * piece]))
    return pieces


def late_tiles_and_rows(parts, held, segments, place, adjoint, total, buffers, payloads, weights, sizes):
    chips, groups, blocks, relations = sizes
    edge, feature = total.shape[1:]
    rows = blocks * edge
    behind = len({j for level, _ in segments for j in level})
    return pl.pallas_call(
        functools.partial(late_kernel, parts, held, segments, sizes),
        out_shape=[
            jax.ShapeDtypeStruct((groups, rows // groups, feature), jnp.bfloat16),
            jax.ShapeDtypeStruct((CORES, relations, rows, feature), jnp.bfloat16),
            jax.ShapeDtypeStruct(total.shape, total.dtype),
        ],
        in_specs=[SMEM] + [VMEM] * 2 + [ANY] * len(buffers) + [VMEM] * (1 + len(payloads)),
        out_specs=[VMEM] * 3,
        scratch_shapes=[
            pltpu.VMEM((behind, rows, feature), jnp.bfloat16),
            pltpu.VMEM((chips, SLOTS, edge), jnp.int32),
            pltpu.SMEM((chips, SLOTS, edge), jnp.int32),
            pltpu.SemaphoreType.DMA((chips,)),
            pltpu.SemaphoreType.DMA((behind, groups)),
        ],
        input_output_aliases={2: 2},
        compiler_params=pltpu.CompilerParams(vmem_limit_bytes=LIMIT),
        cost_estimate=pl.CostEstimate(flops=0, bytes_accessed=1_000_000, transcendentals=0),
        name="late_tiles_and_rows",
    )(place, adjoint, total, *buffers, *payloads, weights)


def turn_kernel(*refs):
    half = len(refs) // 2
    for source, target in zip(refs[:half], refs[half:], strict=True):
        target[...] = source[...].T


def turned(*arrays):
    return pl.pallas_call(
        turn_kernel,
        out_shape=[jax.ShapeDtypeStruct(a.shape[::-1], a.dtype) for a in arrays],
        in_specs=[VMEM] * len(arrays),
        out_specs=[VMEM] * len(arrays),
        compiler_params=pltpu.CompilerParams(vmem_limit_bytes=LIMIT),
        cost_estimate=pl.CostEstimate(flops=0, bytes_accessed=1_000_000, transcendentals=0),
        name="turn_inputs",
    )(*arrays)


def rows_kernel(groups, place_ref, summed, weights_ref, far_ref, kept, sent):
    half = groups // 2
    for spot, value in multiply_rows(place_ref, summed, weights_ref, groups, 0):
        value += far_ref[spot].astype(jnp.float32)

        @pl.when(spot < half)
        def _():
            kept[spot] = value

        @pl.when(spot >= half)
        def _():
            sent[spot - half] = value.astype(sent.dtype)


def row_terms(place, summed, weights, far):
    groups, piece, feature = far.shape
    shape = (groups // 2, piece, feature)
    return pl.pallas_call(
        functools.partial(rows_kernel, groups),
        out_shape=[
            jax.ShapeDtypeStruct(shape, jnp.float32),
            jax.ShapeDtypeStruct(shape, jnp.bfloat16),
        ],
        in_specs=[SMEM, VMEM, VMEM, VMEM],
        out_specs=[VMEM] * 2,
        compiler_params=pltpu.CompilerParams(vmem_limit_bytes=LIMIT),
        cost_estimate=pl.CostEstimate(
            flops=2 * summed.size * feature, bytes_accessed=4_000_000, transcendentals=0
        ),
        name="row_terms",
    )(place, summed, weights, far)


def grad_kernel(chips, place_ref, summed, near_ref, far_ref, grad_far, grad_own):
    chip, core = place_ref[0], place_ref[2]
    _, relations, _, feature = summed.shape
    share = feature // (chips * CORES)
    for r in range(relations):
        grad = jnp.dot(near_ref[...], summed[core, r], preferred_element_type=jnp.float32)
        grad += jnp.dot(far_ref[...], summed[1 - core, r], preferred_element_type=jnp.float32)
        for far in range(CORES):
            out = grad_far if far else grad_own
            for c in range(chips):
                for h in range(CORES):
                    slab = grad[(c * CORES + h) * share : (c * CORES + h + 1) * share]

                    @pl.when(h == (core ^ far))
                    def _():
                        out[chip ^ c, r] = slab.astype(out.dtype)


def grad_terms(place, summed, near, far, chips):
    _, relations, rows, feature = summed.shape
    shape = (chips, relations, feature // (chips * CORES), feature)
    return pl.pallas_call(
        functools.partial(grad_kernel, chips),
        out_shape=[
            jax.ShapeDtypeStruct(shape, jnp.bfloat16),
            jax.ShapeDtypeStruct(shape, jnp.float32),
        ],
        in_specs=[SMEM, VMEM, VMEM, VMEM],
        out_specs=[VMEM] * 2,
        compiler_params=pltpu.CompilerParams(vmem_limit_bytes=LIMIT),
        cost_estimate=pl.CostEstimate(flops=0, bytes_accessed=1_000_000, transcendentals=0),
        name="grad_terms",
    )(place, summed, near, far)


def plane_masks(groups, core):
    masks = [1 << i for i in range(groups.bit_length() - 1)]
    return masks[::-1] if core % CORES else masks


def after(value, *others):
    return lax.optimization_barrier((value, *others))[0]


def on_device(
    out_adjoint,
    layer_input,
    rel_weights,
    self_weight,
    tile_values,
    tile_rel,
    tile_target,
    tile_src,
    tile_dest,
):
    nodes = lax.axis_size("node")
    groups = lax.axis_size("rel")
    chips = nodes // CORES
    node = lax.axis_index("node")
    group = lax.axis_index("rel")
    chip, core = node // CORES, node % CORES
    edge = tile_values.shape[-1]
    rows = layer_input.shape[1]
    blocks = rows // edge
    relations = rel_weights.shape[0]

    def across(value, axis, size, mask):
        return lax.ppermute(value, axis, [(i, i ^ mask) for i in range(size)])

    def to_chip(value, j):
        return across(value, "node", nodes, CORES * j)

    def in_plane(value, step):
        pairs = []
        for g in range(groups):
            for n in range(nodes):
                mask = plane_masks(groups, n)[step]
                pairs.append((g * nodes + n, (g ^ mask) * nodes + n))
        return lax.ppermute(value, ("rel", "node"), pairs)

    own = out_adjoint[0]
    place = jnp.stack([chip, group, core]).astype(jnp.int32)
    details = jnp.stack([tile_dest[0, :, 0], tile_rel[0], tile_target[0], tile_src[0]])

    levels = [
        [j for j in range(chips) if j.bit_count() == count]
        for count in range(chips.bit_length())
    ]
    levels[:2] = [levels[0] + levels[1]]
    steps = groups.bit_length() - 1
    near = layer_input[0]
    far = across(near, "node", nodes, 1)
    mid = chips // 2
    parts = [(0, 0, SLOTS), (mid, 0, HEAD), (mid, HEAD, SLOTS - HEAD)]
    parts = tuple(parts + [(j, 0, SLOTS) for j in range(chips - 1, 0, -1) if j != mid])
    placed = place_tiles(parts, chips, blocks, relations, details, tile_values[0], place)

    by_chip = {0: own}
    for j in levels[0][1:]:
        by_chip[j] = to_chip(own, j)
    head = to_chip(placed[1], mid)
    first = [head, far] + [by_chip[j] for j in levels[0][1:]]
    body = to_chip(after(placed[2], *first), mid)
    payloads = [placed[0], head, body]
    for value, (j, _, _) in list(zip(placed, parts, strict=True))[3:-1]:
        payloads.append(to_chip(after(value, *first), j))
    for level in levels[1:]:
        for j in level:
            bit = j & -j
            by_chip[j] = to_chip(after(by_chip[j ^ bit], *first), bit)

    buffers, segments = [], []
    for n, level in enumerate(levels):
        held = [by_chip[j] for j in level]
        held = held[0] if len(held) == 1 else jnp.concatenate(held)
        if n == 0:
            held = after(held, *first)
        held = [(held, ((0, 0),))]
        for step in range(steps):
            if n:
                merged = jnp.concatenate([value for value, _ in held]) if step else held[0][0]
                if n == 1 and step == steps - 1:
                    payloads.append(to_chip(after(placed[-1], merged), 1))
                    merged = after(merged, body)
                held = [(merged, sum((origins for _, origins in held), ()))]
            masks = [plane_masks(groups, c)[step] for c in range(CORES)]
            held = held + [
                (in_plane(value, step), tuple((a ^ masks[0], b ^ masks[1]) for a, b in origins))
                for value, origins in held
            ]
        for value, origins in held:
            buffers.append(value)
            segments.append((level, origins))
    sizes = (chips, groups, blocks, relations)
    early = [i for i, (j, _, _) in enumerate(parts) if j in (0, mid)]
    late = [i for i in range(len(parts)) if i not in early][::-1]
    split = sum(level == levels[0] for level, _ in segments)
    near, far = turned(near, far)
    adjoint, total = early_tiles(
        tuple(parts[i] for i in early),
        segments[:split],
        after(place, near, far),
        buffers[:split],
        [payloads[i] for i in early],
        sizes,
    )
    rows_far, summed, _ = late_tiles_and_rows(
        tuple(parts[i] for i in late),
        sorted(levels[0]),
        segments[split:],
        place,
        adjoint,
        total,
        buffers[split:],
        [payloads[i] for i in late],
        rel_weights,
        sizes,
    )
    rows_far = across(rows_far, "node", nodes, 1)
    sums, passed = row_terms(place, summed, rel_weights, rows_far)
    for step in range(steps):
        if step:
            half = sums.shape[0] // 2
            sums, passed = sums[:half], sums[half:].astype(jnp.bfloat16)
        sums = sums + in_plane(passed, step).astype(jnp.float32)
    d_source = sums[0] + jnp.einsum(
        "vj,ij->vi", own, self_weight, preferred_element_type=jnp.float32
    )

    grad_far, grad_own = grad_terms(place, summed, near, far, chips)
    grad_far = across(grad_far, "node", nodes, 1)
    grad = grad_own + grad_far.astype(jnp.float32)
    others = [to_chip(grad[j].astype(jnp.bfloat16), j) for j in range(1, chips)]
    rel_weight_grad = grad[0]
    for other in others:
        rel_weight_grad += other.astype(jnp.float32)
    return rel_weight_grad, d_source.astype(jnp.bfloat16)[None]


def solution(mesh):
    return jax.shard_map(
        on_device,
        mesh=mesh,
        in_specs=(
            P("node", "rel", None),
            P("node", None, None),
            P("rel", None, None),
            P(),
            P("rel", "node", None, None),
            P("rel", "node"),
            P("rel", "node"),
            P("rel", "node"),
            P("rel", "node", None),
        ),
        out_specs=(P("rel", "node", None), P("node", "rel", None)),
        check_vma=False,
    )
```

```python
import functools

import jax
import jax.numpy as jnp
from jax import lax
from jax.experimental import pallas as pl
from jax.experimental.pallas import tpu as pltpu
from jax.sharding import PartitionSpec as P

CAPACITY = 8
CORES = 2
SLOTS = CORES * CAPACITY
LIMIT = 24 * 1024 * 1024
HEAD = 3
SMEM = pl.BlockSpec(memory_space=pltpu.SMEM)
VMEM = pl.BlockSpec(memory_space=pltpu.VMEM)
ANY = pl.BlockSpec(memory_space=pl.ANY)


def payload_rows(edge, first, size):
    return size * edge + (SLOTS if first == 0 else 0)


def place_kernel(parts, chips, blocks, relations, *refs):
    given, place_ref, outs = refs[:2], refs[2], refs[3 : 3 + len(parts)]
    details, tiles_ref, order, count, sem = refs[3 + len(parts) :]
    copies = [
        pltpu.make_async_copy(given[0], details, sem.at[0]),
        pltpu.make_async_copy(given[1], tiles_ref, sem.at[1]),
    ]
    for copy in copies:
        copy.start()
    chip = place_ref[0]
    edge = tiles_ref.shape[-1]
    for j in range(chips):
        count[j] = 0
    for s in range(chips * SLOTS):
        order[s] = 0
    copies[0].wait()

    def rank(t, carry):
        j = (details[0, t] // CORES) ^ chip
        p = count[j]
        order[j * SLOTS + p] = t
        count[j] = p + 1
        return carry

    lax.fori_loop(0, details.shape[1], rank, 0)
    copies[1].wait()
    lane = lax.broadcasted_iota(jnp.int32, (SLOTS, edge), 1)
    row = lax.broadcasted_iota(jnp.int32, (SLOTS, edge), 0)
    for out, (j, first, size) in zip(outs, parts, strict=True):
        for p in range(size):
            tile = tiles_ref[order[j * SLOTS + first + p]]
            full = first + p < count[j]
            out[p * edge : (p + 1) * edge, :] = jnp.where(full, tile, jnp.zeros_like(tile))
        if first == 0:
            codes = jnp.zeros((SLOTS, edge), jnp.int32)
            for p in range(SLOTS):
                t = order[j * SLOTS + p]
                bucket = (details[0, t] % CORES) * relations + details[1, t]
                code = jnp.where(lane == 0, bucket * blocks + details[3, t], details[2, t])
                codes = jnp.where(row == p, code, codes)
            out[size * edge :, :] = codes.astype(jnp.float32).astype(jnp.bfloat16)


def place_tiles(parts, chips, blocks, relations, details, tiles, place):
    edge = tiles.shape[-1]
    shapes = [
        jax.ShapeDtypeStruct((payload_rows(edge, first, size), edge), tiles.dtype)
        for _, first, size in parts
    ]
    return pl.pallas_call(
        functools.partial(place_kernel, parts, chips, blocks, relations),
        out_shape=shapes,
        in_specs=[ANY] * 2 + [SMEM],
        out_specs=[VMEM] * len(shapes),
        scratch_shapes=[
            pltpu.SMEM(details.shape, jnp.int32),
            pltpu.VMEM(tiles.shape, tiles.dtype),
            pltpu.SMEM((chips * SLOTS,), jnp.int32),
            pltpu.SMEM((chips,), jnp.int32),
            pltpu.SemaphoreType.DMA((2,)),
        ],
        compiler_params=pltpu.CompilerParams(vmem_limit_bytes=LIMIT),
        cost_estimate=pl.CostEstimate(flops=0, bytes_accessed=4_000_000, transcendentals=0),
        name="place_tiles",
    )(details, tiles, place)


def read_codes(parts, payloads, vector, codes, sem):
    copies = {}
    for payload, (j, first, size) in zip(payloads, parts, strict=True):
        if first == 0:
            last = payload[payload.shape[0] - SLOTS :, :]
            vector[j] = last.astype(jnp.float32).astype(jnp.int32)
            copies[j] = pltpu.make_async_copy(vector.at[j], codes.at[j], sem.at[j])
            copies[j].start()
    return copies


def gather_moves(buffers, segments, place_ref, groups, adjoint, landed):
    group, core = place_ref[1], place_ref[2]
    piece = adjoint.shape[1] // groups
    where = sorted({j for level, _ in segments for j in level})
    moves = {j: [] for j in where}
    for buffer, (level, origins) in zip(buffers, segments, strict=True):
        for q, origin in enumerate(origins):
            start = jnp.where(core == 0, origin[0], origin[1]) ^ group
            start = pl.multiple_of(start * piece, piece)
            for n, j in enumerate(level):
                moves[j].append(
                    pltpu.make_async_copy(
                        buffer.at[pl.ds((q * len(level) + n) * piece, piece)],
                        adjoint.at[where.index(j), pl.ds(start, piece)],
                        landed.at[where.index(j), len(moves[j])],
                    )
                )
                moves[j][-1].start()
    return where, moves


def add_tiles(payload, j, first, size, adjoint, total, codes):
    edge = payload.shape[-1]
    unroll = next(u for u in range(min(size, 16), 0, -1) if size % u == 0)
    if unroll == 1:
        unroll = size

    def some(i, carry):
        for u in range(unroll):
            p = i * unroll + u
            row = pl.multiple_of(codes[j, first + p, 1] * edge, edge)
            partial = lax.dot_general(
                payload[pl.ds(pl.multiple_of(p * edge, edge), edge), :],
                adjoint[pl.ds(row, edge), :],
                (((0,), (0,)), ((), ())),
                preferred_element_type=jnp.float32,
            )
            total[codes[j, first + p, 0]] += partial.astype(jnp.bfloat16).astype(jnp.float32)
        return carry

    lax.fori_loop(0, size // unroll, some, 0)


def early_kernel(parts, segments, groups, place_ref, *refs):
    buffers, refs = refs[: len(segments)], refs[len(segments) :]
    payloads, refs = refs[: len(parts)], refs[len(parts) :]
    adjoint, total, vector, codes, sem, landed = refs
    where, moves = gather_moves(buffers, segments, place_ref, groups, adjoint, landed)
    copies = read_codes(parts, payloads, vector, codes, sem)
    total[...] = jnp.zeros_like(total)
    for j in where:
        for move in moves[j]:
            move.wait()
    for payload, (j, first, size) in zip(payloads, parts, strict=True):
        if first == 0:
            copies[j].wait()
        add_tiles(payload, j, first, size, adjoint.at[where.index(j)], total, codes)


def early_tiles(parts, segments, place, buffers, payloads, sizes):
    chips, groups, blocks, relations = sizes
    edge, feature = payloads[0].shape[-1], buffers[0].shape[-1]
    held = len({j for level, _ in segments for j in level})
    return pl.pallas_call(
        functools.partial(early_kernel, parts, segments, groups),
        out_shape=[
            jax.ShapeDtypeStruct((held, blocks * edge, feature), jnp.bfloat16),
            jax.ShapeDtypeStruct((CORES * relations * blocks, edge, feature), jnp.float32),
        ],
        in_specs=[SMEM] + [ANY] * len(buffers) + [VMEM] * len(payloads),
        out_specs=[VMEM] * 2,
        scratch_shapes=[
            pltpu.VMEM((chips, SLOTS, edge), jnp.int32),
            pltpu.SMEM((chips, SLOTS, edge), jnp.int32),
            pltpu.SemaphoreType.DMA((chips,)),
            pltpu.SemaphoreType.DMA((held, groups)),
        ],
        compiler_params=pltpu.CompilerParams(vmem_limit_bytes=LIMIT),
        cost_estimate=pl.CostEstimate(flops=0, bytes_accessed=1_000_000, transcendentals=0),
        name="early_tiles",
    )(place, *buffers, *payloads)


def late_kernel(parts, held, segments, sizes, place_ref, adjoint, before, *refs):
    chips, groups, blocks, relations = sizes
    buffers, refs = refs[: len(segments)], refs[len(segments) :]
    payloads, refs = refs[: len(parts)], refs[len(parts) :]
    weights_ref, rows_far, summed, total, late, vector, codes, sem, landed = refs
    edge = payloads[0].shape[-1]
    where, moves = gather_moves(buffers, segments, place_ref, groups, late, landed)
    copies = read_codes(parts, payloads, vector, codes, sem)
    for payload, (j, first, size) in zip(payloads, parts, strict=True):
        if first == 0:
            copies[j].wait()
            for move in moves.get(j, []):
                move.wait()
        shard = late.at[where.index(j)] if j in where else adjoint.at[held.index(j)]
        add_tiles(payload, j, first, size, shard, total, codes)

    for h in range(CORES):
        for r in range(relations):
            part = total[pl.ds((h * relations + r) * blocks, blocks)].astype(jnp.bfloat16)
            part = part.reshape(blocks * edge, part.shape[-1])
            rows, feature = part.shape
            summed[h * rows : (h + 1) * rows, r * feature : (r + 1) * feature] = part
    for spot, value in multiply_rows(place_ref, summed, weights_ref, groups, 1):
        rows_far[spot] = value.astype(rows_far.dtype)


def multiply_rows(place_ref, summed, weights_ref, groups, far):
    group, core = place_ref[1], place_ref[2]
    rows = summed.shape[0] // CORES
    piece = rows // groups
    steps = groups.bit_length() - 1
    value = jnp.dot(
        summed[pl.ds(pl.multiple_of((core ^ far) * rows, rows), rows), :],
        weights_ref[...],
        preferred_element_type=jnp.float32,
    )
    pieces = []
    for q in range(groups):
        mask = group ^ q
        spot = [0, 0]
        for step in range(steps):
            for c in range(CORES):
                bit = plane_masks(groups, c)[step].bit_length() - 1
                spot[c] = spot[c] + (((mask >> bit) & 1) << (steps - 1 - step))
        spot = jnp.where((core ^ far) == 0, spot[0], spot[1])
        pieces.append((spot, value[q * piece : (q + 1) * piece]))
    return pieces


def late_tiles_and_rows(parts, held, segments, place, adjoint, total, buffers, payloads, weights, sizes):
    chips, groups, blocks, relations = sizes
    edge, feature = total.shape[1:]
    rows = blocks * edge
    behind = len({j for level, _ in segments for j in level})
    return pl.pallas_call(
        functools.partial(late_kernel, parts, held, segments, sizes),
        out_shape=[
            jax.ShapeDtypeStruct((groups, rows // groups, feature), jnp.bfloat16),
            jax.ShapeDtypeStruct((CORES * rows, relations * feature), jnp.bfloat16),
            jax.ShapeDtypeStruct(total.shape, total.dtype),
        ],
        in_specs=[SMEM] + [VMEM] * 2 + [ANY] * len(buffers) + [VMEM] * (1 + len(payloads)),
        out_specs=[VMEM] * 3,
        scratch_shapes=[
            pltpu.VMEM((behind, rows, feature), jnp.bfloat16),
            pltpu.VMEM((chips, SLOTS, edge), jnp.int32),
            pltpu.SMEM((chips, SLOTS, edge), jnp.int32),
            pltpu.SemaphoreType.DMA((chips,)),
            pltpu.SemaphoreType.DMA((behind, groups)),
        ],
        input_output_aliases={2: 2},
        compiler_params=pltpu.CompilerParams(vmem_limit_bytes=LIMIT),
        cost_estimate=pl.CostEstimate(flops=0, bytes_accessed=1_000_000, transcendentals=0),
        name="late_tiles_and_rows",
    )(place, adjoint, total, *buffers, *payloads, weights)


def turn_kernel(place_ref, near_ref, far_ref, weights_ref, inputs, weights):
    core = place_ref[2]
    rows, feature = near_ref.shape
    near, far = near_ref[...].T, far_ref[...].T
    for c in range(CORES):

        @pl.when(core == c)
        def _():
            inputs[:, c * rows : (c + 1) * rows] = near
            inputs[:, (1 - c) * rows : (2 - c) * rows] = far

    for r in range(weights_ref.shape[0]):
        weights[r * feature : (r + 1) * feature, :] = weights_ref[r].T


def turned(place, near, far, weights):
    rows, feature = near.shape
    return pl.pallas_call(
        turn_kernel,
        out_shape=[
            jax.ShapeDtypeStruct((feature, CORES * rows), near.dtype),
            jax.ShapeDtypeStruct((weights.shape[0] * feature, feature), weights.dtype),
        ],
        in_specs=[SMEM] + [VMEM] * 3,
        out_specs=[VMEM] * 2,
        compiler_params=pltpu.CompilerParams(vmem_limit_bytes=LIMIT),
        cost_estimate=pl.CostEstimate(flops=0, bytes_accessed=1_000_000, transcendentals=0),
        name="turn_inputs",
    )(place, near, far, weights)


def rows_kernel(groups, place_ref, summed, weights_ref, far_ref, kept, sent):
    half = groups // 2
    for spot, value in multiply_rows(place_ref, summed, weights_ref, groups, 0):
        value += far_ref[spot].astype(jnp.float32)

        @pl.when(spot < half)
        def _():
            kept[spot] = value

        @pl.when(spot >= half)
        def _():
            sent[spot - half] = value.astype(sent.dtype)


def row_terms(place, summed, weights, far):
    groups, piece, feature = far.shape
    shape = (groups // 2, piece, feature)
    return pl.pallas_call(
        functools.partial(rows_kernel, groups),
        out_shape=[
            jax.ShapeDtypeStruct(shape, jnp.float32),
            jax.ShapeDtypeStruct(shape, jnp.bfloat16),
        ],
        in_specs=[SMEM, VMEM, VMEM, VMEM],
        out_specs=[VMEM] * 2,
        compiler_params=pltpu.CompilerParams(vmem_limit_bytes=LIMIT),
        cost_estimate=pl.CostEstimate(
            flops=2 * summed.size * feature, bytes_accessed=4_000_000, transcendentals=0
        ),
        name="row_terms",
    )(place, summed, weights, far)


def grad_kernel(chips, relations, place_ref, summed, inputs_ref, grad_far, grad_own):
    chip, core = place_ref[0], place_ref[2]
    feature = inputs_ref.shape[0]
    share = feature // (chips * CORES)
    grad = jnp.dot(inputs_ref[...], summed[...], preferred_element_type=jnp.float32)
    for r in range(relations):
        for far in range(CORES):
            out = grad_far if far else grad_own
            for c in range(chips):
                for h in range(CORES):
                    start = (c * CORES + h) * share
                    slab = grad[start : start + share, r * feature : (r + 1) * feature]

                    @pl.when(h == (core ^ far))
                    def _():
                        out[chip ^ c, r] = slab.astype(out.dtype)


def grad_terms(place, summed, inputs, chips):
    feature = inputs.shape[0]
    relations = summed.shape[1] // feature
    shape = (chips, relations, feature // (chips * CORES), feature)
    return pl.pallas_call(
        functools.partial(grad_kernel, chips, relations),
        out_shape=[
            jax.ShapeDtypeStruct(shape, jnp.bfloat16),
            jax.ShapeDtypeStruct(shape, jnp.float32),
        ],
        in_specs=[SMEM, VMEM, VMEM],
        out_specs=[VMEM] * 2,
        compiler_params=pltpu.CompilerParams(vmem_limit_bytes=LIMIT),
        cost_estimate=pl.CostEstimate(flops=0, bytes_accessed=1_000_000, transcendentals=0),
        name="grad_terms",
    )(place, summed, inputs)


def plane_masks(groups, core):
    masks = [1 << i for i in range(groups.bit_length() - 1)]
    return masks[::-1] if core % CORES else masks


def after(value, *others):
    return lax.optimization_barrier((value, *others))[0]


def on_device(
    out_adjoint,
    layer_input,
    rel_weights,
    self_weight,
    tile_values,
    tile_rel,
    tile_target,
    tile_src,
    tile_dest,
):
    nodes = lax.axis_size("node")
    groups = lax.axis_size("rel")
    chips = nodes // CORES
    node = lax.axis_index("node")
    group = lax.axis_index("rel")
    chip, core = node // CORES, node % CORES
    edge = tile_values.shape[-1]
    rows = layer_input.shape[1]
    blocks = rows // edge
    relations = rel_weights.shape[0]

    def across(value, axis, size, mask):
        return lax.ppermute(value, axis, [(i, i ^ mask) for i in range(size)])

    def to_chip(value, j):
        return across(value, "node", nodes, CORES * j)

    def in_plane(value, step):
        pairs = []
        for g in range(groups):
            for n in range(nodes):
                mask = plane_masks(groups, n)[step]
                pairs.append((g * nodes + n, (g ^ mask) * nodes + n))
        return lax.ppermute(value, ("rel", "node"), pairs)

    own = out_adjoint[0]
    place = jnp.stack([chip, group, core]).astype(jnp.int32)
    details = jnp.stack([tile_dest[0, :, 0], tile_rel[0], tile_target[0], tile_src[0]])

    levels = [
        [j for j in range(chips) if j.bit_count() == count]
        for count in range(chips.bit_length())
    ]
    levels[:2] = [levels[0] + levels[1]]
    steps = groups.bit_length() - 1
    near = layer_input[0]
    far = across(near, "node", nodes, 1)
    mid = chips // 2
    parts = [(0, 0, SLOTS), (mid, 0, HEAD), (mid, HEAD, SLOTS - HEAD)]
    parts = tuple(parts + [(j, 0, SLOTS) for j in range(chips - 1, 0, -1) if j != mid])
    placed = place_tiles(parts, chips, blocks, relations, details, tile_values[0], place)

    by_chip = {0: own}
    for j in levels[0][1:]:
        by_chip[j] = to_chip(own, j)
    head = to_chip(placed[1], mid)
    first = [head, far] + [by_chip[j] for j in levels[0][1:]]
    body = to_chip(after(placed[2], *first), mid)
    payloads = [placed[0], head, body]
    for value, (j, _, _) in list(zip(placed, parts, strict=True))[3:-1]:
        payloads.append(to_chip(after(value, *first), j))
    for level in levels[1:]:
        for j in level:
            bit = j & -j
            by_chip[j] = to_chip(after(by_chip[j ^ bit], *first), bit)

    buffers, segments = [], []
    for n, level in enumerate(levels):
        held = [by_chip[j] for j in level]
        held = held[0] if len(held) == 1 else jnp.concatenate(held)
        if n == 0:
            held = after(held, *first)
        held = [(held, ((0, 0),))]
        for step in range(steps):
            if n:
                merged = jnp.concatenate([value for value, _ in held]) if step else held[0][0]
                if n == 1 and step == steps - 1:
                    payloads.append(to_chip(after(placed[-1], merged), 1))
                    merged = after(merged, body)
                held = [(merged, sum((origins for _, origins in held), ()))]
            masks = [plane_masks(groups, c)[step] for c in range(CORES)]
            held = held + [
                (in_plane(value, step), tuple((a ^ masks[0], b ^ masks[1]) for a, b in origins))
                for value, origins in held
            ]
        for value, origins in held:
            buffers.append(value)
            segments.append((level, origins))
    sizes = (chips, groups, blocks, relations)
    early = [i for i, (j, _, _) in enumerate(parts) if j in (0, mid)]
    late = [i for i in range(len(parts)) if i not in early][::-1]
    split = sum(level == levels[0] for level, _ in segments)
    inputs, weights = turned(place, near, far, rel_weights)
    adjoint, total = early_tiles(
        tuple(parts[i] for i in early),
        segments[:split],
        after(place, inputs, weights),
        buffers[:split],
        [payloads[i] for i in early],
        sizes,
    )
    rows_far, summed, _ = late_tiles_and_rows(
        tuple(parts[i] for i in late),
        sorted(levels[0]),
        segments[split:],
        place,
        adjoint,
        total,
        buffers[split:],
        [payloads[i] for i in late],
        weights,
        sizes,
    )
    rows_far = across(rows_far, "node", nodes, 1)
    sums, passed = row_terms(place, summed, weights, rows_far)
    for step in range(steps):
        if step:
            half = sums.shape[0] // 2
            sums, passed = sums[:half], sums[half:].astype(jnp.bfloat16)
        sums = sums + in_plane(passed, step).astype(jnp.float32)
    d_source = sums[0] + jnp.einsum(
        "vj,ij->vi", own, self_weight, preferred_element_type=jnp.float32
    )

    grad_far, grad_own = grad_terms(place, summed, inputs, chips)
    grad_far = across(grad_far, "node", nodes, 1)
    grad = grad_own + grad_far.astype(jnp.float32)
    others = [to_chip(grad[j].astype(jnp.bfloat16), j) for j in range(chips - 1, 0, -1)]
    rel_weight_grad = grad[0]
    for other in others:
        rel_weight_grad += other.astype(jnp.float32)
    return rel_weight_grad, d_source.astype(jnp.bfloat16)[None]


def solution(mesh):
    return jax.shard_map(
        on_device,
        mesh=mesh,
        in_specs=(
            P("node", "rel", None),
            P("node", None, None),
            P("rel", None, None),
            P(),
            P("rel", "node", None, None),
            P("rel", "node"),
            P("rel", "node"),
            P("rel", "node"),
            P("rel", "node", None),
        ),
        out_specs=(P("rel", "node", None), P("node", "rel", None)),
        check_vma=False,
    )
```

```python
import functools

import jax
import jax.numpy as jnp
from jax import lax
from jax.experimental import pallas as pl
from jax.experimental.pallas import tpu as pltpu
from jax.sharding import PartitionSpec as P

CAPACITY = 8
CORES = 2
SLOTS = CORES * CAPACITY
LIMIT = 24 * 1024 * 1024
HEAD = 3
SMEM = pl.BlockSpec(memory_space=pltpu.SMEM)
VMEM = pl.BlockSpec(memory_space=pltpu.VMEM)
ANY = pl.BlockSpec(memory_space=pl.ANY)


def payload_rows(edge, first, size):
    return size * edge + (SLOTS if first == 0 else 0)


def place_kernel(parts, chips, blocks, relations, *refs):
    given, place_ref, outs = refs[:2], refs[2], refs[3 : 3 + len(parts)]
    details, tiles_ref, order, count, sem = refs[3 + len(parts) :]
    copies = [
        pltpu.make_async_copy(given[0], details, sem.at[0]),
        pltpu.make_async_copy(given[1], tiles_ref, sem.at[1]),
    ]
    for copy in copies:
        copy.start()
    chip = place_ref[0]
    edge = tiles_ref.shape[-1]
    for j in range(chips):
        count[j] = 0
    for s in range(chips * SLOTS):
        order[s] = 0
    copies[0].wait()

    def rank(t, carry):
        j = (details[0, t] // CORES) ^ chip
        p = count[j]
        order[j * SLOTS + p] = t
        count[j] = p + 1
        return carry

    lax.fori_loop(0, details.shape[1], rank, 0)
    copies[1].wait()
    lane = lax.broadcasted_iota(jnp.int32, (SLOTS, edge), 1)
    row = lax.broadcasted_iota(jnp.int32, (SLOTS, edge), 0)
    for out, (j, first, size) in zip(outs, parts, strict=True):
        for p in range(size):
            tile = tiles_ref[order[j * SLOTS + first + p]]
            full = first + p < count[j]
            out[p * edge : (p + 1) * edge, :] = jnp.where(full, tile, jnp.zeros_like(tile))
        if first == 0:
            codes = jnp.zeros((SLOTS, edge), jnp.int32)
            for p in range(SLOTS):
                t = order[j * SLOTS + p]
                bucket = (details[0, t] % CORES) * relations + details[1, t]
                code = jnp.where(lane == 0, bucket * blocks + details[3, t], details[2, t])
                codes = jnp.where(row == p, code, codes)
            out[size * edge :, :] = codes.astype(jnp.float32).astype(jnp.bfloat16)


def place_tiles(parts, chips, blocks, relations, details, tiles, place):
    edge = tiles.shape[-1]
    shapes = [
        jax.ShapeDtypeStruct((payload_rows(edge, first, size), edge), tiles.dtype)
        for _, first, size in parts
    ]
    return pl.pallas_call(
        functools.partial(place_kernel, parts, chips, blocks, relations),
        out_shape=shapes,
        in_specs=[ANY] * 2 + [SMEM],
        out_specs=[VMEM] * len(shapes),
        scratch_shapes=[
            pltpu.SMEM(details.shape, jnp.int32),
            pltpu.VMEM(tiles.shape, tiles.dtype),
            pltpu.SMEM((chips * SLOTS,), jnp.int32),
            pltpu.SMEM((chips,), jnp.int32),
            pltpu.SemaphoreType.DMA((2,)),
        ],
        compiler_params=pltpu.CompilerParams(vmem_limit_bytes=LIMIT),
        cost_estimate=pl.CostEstimate(flops=0, bytes_accessed=4_000_000, transcendentals=0),
        name="place_tiles",
    )(details, tiles, place)


def read_codes(parts, payloads, vector, codes, sem):
    copies = {}
    for payload, (j, first, size) in zip(payloads, parts, strict=True):
        if first == 0:
            last = payload[payload.shape[0] - SLOTS :, :]
            vector[j] = last.astype(jnp.float32).astype(jnp.int32)
            copies[j] = pltpu.make_async_copy(vector.at[j], codes.at[j], sem.at[j])
            copies[j].start()
    return copies


def gather_moves(buffers, segments, place_ref, groups, adjoint, landed):
    group, core = place_ref[1], place_ref[2]
    piece = adjoint.shape[1] // groups
    where = sorted({j for level, _ in segments for j in level})
    moves = {j: [] for j in where}
    for buffer, (level, origins) in zip(buffers, segments, strict=True):
        for q, origin in enumerate(origins):
            start = jnp.where(core == 0, origin[0], origin[1]) ^ group
            start = pl.multiple_of(start * piece, piece)
            for n, j in enumerate(level):
                moves[j].append(
                    pltpu.make_async_copy(
                        buffer.at[pl.ds((q * len(level) + n) * piece, piece)],
                        adjoint.at[where.index(j), pl.ds(start, piece)],
                        landed.at[where.index(j), len(moves[j])],
                    )
                )
                moves[j][-1].start()
    return where, moves


def add_tiles(payload, j, first, size, adjoint, total, codes):
    edge = payload.shape[-1]
    unroll = next(u for u in range(min(size, 16), 0, -1) if size % u == 0)
    if unroll == 1:
        unroll = size

    def some(i, carry):
        for u in range(unroll):
            p = i * unroll + u
            row = pl.multiple_of(codes[j, first + p, 1] * edge, edge)
            partial = lax.dot_general(
                payload[pl.ds(pl.multiple_of(p * edge, edge), edge), :],
                adjoint[pl.ds(row, edge), :],
                (((0,), (0,)), ((), ())),
                preferred_element_type=jnp.float32,
            )
            total[codes[j, first + p, 0]] += partial.astype(jnp.bfloat16).astype(jnp.float32)
        return carry

    lax.fori_loop(0, size // unroll, some, 0)


def early_kernel(parts, segments, groups, place_ref, *refs):
    buffers, refs = refs[: len(segments)], refs[len(segments) :]
    payloads, refs = refs[: len(parts)], refs[len(parts) :]
    adjoint, total, vector, codes, sem, landed = refs
    where, moves = gather_moves(buffers, segments, place_ref, groups, adjoint, landed)
    copies = read_codes(parts, payloads, vector, codes, sem)
    total[...] = jnp.zeros_like(total)
    for j in where:
        for move in moves[j]:
            move.wait()
    for payload, (j, first, size) in zip(payloads, parts, strict=True):
        if first == 0:
            copies[j].wait()
        add_tiles(payload, j, first, size, adjoint.at[where.index(j)], total, codes)


def early_tiles(parts, segments, place, buffers, payloads, sizes):
    chips, groups, blocks, relations = sizes
    edge, feature = payloads[0].shape[-1], buffers[0].shape[-1]
    held = len({j for level, _ in segments for j in level})
    return pl.pallas_call(
        functools.partial(early_kernel, parts, segments, groups),
        out_shape=[
            jax.ShapeDtypeStruct((held, blocks * edge, feature), jnp.bfloat16),
            jax.ShapeDtypeStruct((CORES * relations * blocks, edge, feature), jnp.float32),
        ],
        in_specs=[SMEM] + [ANY] * len(buffers) + [VMEM] * len(payloads),
        out_specs=[VMEM] * 2,
        scratch_shapes=[
            pltpu.VMEM((chips, SLOTS, edge), jnp.int32),
            pltpu.SMEM((chips, SLOTS, edge), jnp.int32),
            pltpu.SemaphoreType.DMA((chips,)),
            pltpu.SemaphoreType.DMA((held, groups)),
        ],
        compiler_params=pltpu.CompilerParams(vmem_limit_bytes=LIMIT),
        cost_estimate=pl.CostEstimate(flops=0, bytes_accessed=1_000_000, transcendentals=0),
        name="early_tiles",
    )(place, *buffers, *payloads)


def late_kernel(parts, held, segments, sizes, place_ref, adjoint, before, *refs):
    chips, groups, blocks, relations = sizes
    buffers, refs = refs[: len(segments)], refs[len(segments) :]
    payloads, refs = refs[: len(parts)], refs[len(parts) :]
    weights_ref, rows_far, summed, total, late, vector, codes, sem, landed = refs
    edge = payloads[0].shape[-1]
    where, moves = gather_moves(buffers, segments, place_ref, groups, late, landed)
    copies = read_codes(parts, payloads, vector, codes, sem)
    for payload, (j, first, size) in zip(payloads, parts, strict=True):
        if first == 0:
            copies[j].wait()
            for move in moves.get(j, []):
                move.wait()
        shard = late.at[where.index(j)] if j in where else adjoint.at[held.index(j)]
        add_tiles(payload, j, first, size, shard, total, codes)

    for h in range(CORES):
        for r in range(relations):
            part = total[pl.ds((h * relations + r) * blocks, blocks)].astype(jnp.bfloat16)
            part = part.reshape(blocks * edge, part.shape[-1])
            rows, feature = part.shape
            summed[h * rows : (h + 1) * rows, r * feature : (r + 1) * feature] = part
    for spot, value in multiply_rows(place_ref, summed, weights_ref, groups, 1):
        rows_far[spot] = value.astype(rows_far.dtype)


def multiply_rows(place_ref, summed, weights_ref, groups, far):
    group, core = place_ref[1], place_ref[2]
    rows = summed.shape[0] // CORES
    piece = rows // groups
    steps = groups.bit_length() - 1
    value = jnp.dot(
        summed[pl.ds(pl.multiple_of((core ^ far) * rows, rows), rows), :],
        weights_ref[...],
        preferred_element_type=jnp.float32,
    )
    pieces = []
    for q in range(groups):
        mask = group ^ q
        spot = [0, 0]
        for step in range(steps):
            for c in range(CORES):
                bit = plane_masks(groups, c)[step].bit_length() - 1
                spot[c] = spot[c] + (((mask >> bit) & 1) << (steps - 1 - step))
        spot = jnp.where((core ^ far) == 0, spot[0], spot[1])
        pieces.append((spot, value[q * piece : (q + 1) * piece]))
    return pieces


def late_tiles_and_rows(parts, held, segments, place, adjoint, total, buffers, payloads, weights, sizes):
    chips, groups, blocks, relations = sizes
    edge, feature = total.shape[1:]
    rows = blocks * edge
    behind = len({j for level, _ in segments for j in level})
    return pl.pallas_call(
        functools.partial(late_kernel, parts, held, segments, sizes),
        out_shape=[
            jax.ShapeDtypeStruct((groups, rows // groups, feature), jnp.bfloat16),
            jax.ShapeDtypeStruct((CORES * rows, relations * feature), jnp.bfloat16),
            jax.ShapeDtypeStruct(total.shape, total.dtype),
        ],
        in_specs=[SMEM] + [VMEM] * 2 + [ANY] * len(buffers) + [VMEM] * (1 + len(payloads)),
        out_specs=[VMEM] * 3,
        scratch_shapes=[
            pltpu.VMEM((behind, rows, feature), jnp.bfloat16),
            pltpu.VMEM((chips, SLOTS, edge), jnp.int32),
            pltpu.SMEM((chips, SLOTS, edge), jnp.int32),
            pltpu.SemaphoreType.DMA((chips,)),
            pltpu.SemaphoreType.DMA((behind, groups)),
        ],
        input_output_aliases={2: 2},
        compiler_params=pltpu.CompilerParams(vmem_limit_bytes=LIMIT),
        cost_estimate=pl.CostEstimate(flops=0, bytes_accessed=1_000_000, transcendentals=0),
        name="late_tiles_and_rows",
    )(place, adjoint, total, *buffers, *payloads, weights)


def turn_kernel(place_ref, near_ref, far_ref, weights_ref, inputs, weights):
    core = place_ref[2]
    rows, feature = near_ref.shape
    near, far = near_ref[...].T, far_ref[...].T
    for c in range(CORES):

        @pl.when(core == c)
        def _():
            inputs[:, c * rows : (c + 1) * rows] = near
            inputs[:, (1 - c) * rows : (2 - c) * rows] = far

    for r in range(weights_ref.shape[0]):
        weights[r * feature : (r + 1) * feature, :] = weights_ref[r].T


def turned(place, near, far, weights):
    rows, feature = near.shape
    return pl.pallas_call(
        turn_kernel,
        out_shape=[
            jax.ShapeDtypeStruct((feature, CORES * rows), near.dtype),
            jax.ShapeDtypeStruct((weights.shape[0] * feature, feature), weights.dtype),
        ],
        in_specs=[SMEM] + [VMEM] * 3,
        out_specs=[VMEM] * 2,
        compiler_params=pltpu.CompilerParams(vmem_limit_bytes=LIMIT),
        cost_estimate=pl.CostEstimate(flops=0, bytes_accessed=1_000_000, transcendentals=0),
        name="turn_inputs",
    )(place, near, far, weights)


def rows_kernel(groups, place_ref, summed, weights_ref, far_ref, kept, sent):
    half = groups // 2
    for spot, value in multiply_rows(place_ref, summed, weights_ref, groups, 0):
        value += far_ref[spot].astype(jnp.float32)

        @pl.when(spot < half)
        def _():
            kept[spot] = value

        @pl.when(spot >= half)
        def _():
            sent[spot - half] = value.astype(sent.dtype)


def row_terms(place, summed, weights, far):
    groups, piece, feature = far.shape
    shape = (groups // 2, piece, feature)
    return pl.pallas_call(
        functools.partial(rows_kernel, groups),
        out_shape=[
            jax.ShapeDtypeStruct(shape, jnp.float32),
            jax.ShapeDtypeStruct(shape, jnp.bfloat16),
        ],
        in_specs=[SMEM, VMEM, VMEM, VMEM],
        out_specs=[VMEM] * 2,
        compiler_params=pltpu.CompilerParams(vmem_limit_bytes=LIMIT),
        cost_estimate=pl.CostEstimate(
            flops=2 * summed.size * feature, bytes_accessed=4_000_000, transcendentals=0
        ),
        name="row_terms",
    )(place, summed, weights, far)


def grad_kernel(chips, relations, place_ref, summed, inputs_ref, grad_far, grad_own):
    chip, core = place_ref[0], place_ref[2]
    feature = inputs_ref.shape[0]
    share = feature // (chips * CORES)
    grad = jnp.dot(inputs_ref[...], summed[...], preferred_element_type=jnp.float32)
    for r in range(relations):
        for far in range(CORES):
            out = grad_far if far else grad_own
            for c in range(chips):
                for h in range(CORES):
                    start = (c * CORES + h) * share
                    slab = grad[start : start + share, r * feature : (r + 1) * feature]

                    @pl.when(h == (core ^ far))
                    def _():
                        out[chip ^ c, r] = slab.astype(out.dtype)


def grad_terms(place, summed, inputs, chips):
    feature = inputs.shape[0]
    relations = summed.shape[1] // feature
    shape = (chips, relations, feature // (chips * CORES), feature)
    return pl.pallas_call(
        functools.partial(grad_kernel, chips, relations),
        out_shape=[
            jax.ShapeDtypeStruct(shape, jnp.bfloat16),
            jax.ShapeDtypeStruct(shape, jnp.float32),
        ],
        in_specs=[SMEM, VMEM, VMEM],
        out_specs=[VMEM] * 2,
        compiler_params=pltpu.CompilerParams(vmem_limit_bytes=LIMIT),
        cost_estimate=pl.CostEstimate(flops=0, bytes_accessed=1_000_000, transcendentals=0),
        name="grad_terms",
    )(place, summed, inputs)


def plane_masks(groups, core):
    masks = [1 << i for i in range(groups.bit_length() - 1)]
    return masks[::-1] if core % CORES else masks


def after(value, *others):
    return lax.optimization_barrier((value, *others))[0]


def on_device(
    out_adjoint,
    layer_input,
    rel_weights,
    self_weight,
    tile_values,
    tile_rel,
    tile_target,
    tile_src,
    tile_dest,
):
    nodes = lax.axis_size("node")
    groups = lax.axis_size("rel")
    chips = nodes // CORES
    node = lax.axis_index("node")
    group = lax.axis_index("rel")
    chip, core = node // CORES, node % CORES
    edge = tile_values.shape[-1]
    rows = layer_input.shape[1]
    blocks = rows // edge
    relations = rel_weights.shape[0]

    def across(value, axis, size, mask):
        return lax.ppermute(value, axis, [(i, i ^ mask) for i in range(size)])

    def to_chip(value, j):
        return across(value, "node", nodes, CORES * j)

    def in_plane(value, step):
        pairs = []
        for g in range(groups):
            for n in range(nodes):
                mask = plane_masks(groups, n)[step]
                pairs.append((g * nodes + n, (g ^ mask) * nodes + n))
        return lax.ppermute(value, ("rel", "node"), pairs)

    own = out_adjoint[0]
    place = jnp.stack([chip, group, core]).astype(jnp.int32)
    details = jnp.stack([tile_dest[0, :, 0], tile_rel[0], tile_target[0], tile_src[0]])

    levels = [
        [j for j in range(chips) if j.bit_count() == count]
        for count in range(chips.bit_length())
    ]
    levels[:2] = [levels[0] + levels[1]]
    steps = groups.bit_length() - 1
    near = layer_input[0]
    far = across(near, "node", nodes, 1)
    mid = chips // 2
    parts = [(0, 0, SLOTS), (mid, 0, HEAD), (mid, HEAD, SLOTS - HEAD)]
    parts = tuple(parts + [(j, 0, SLOTS) for j in range(chips - 1, 0, -1) if j != mid])
    placed = place_tiles(parts, chips, blocks, relations, details, tile_values[0], place)

    by_chip = {0: own}
    for j in levels[0][1:]:
        by_chip[j] = to_chip(own, j)
    head = to_chip(placed[1], mid)
    first = [head] + [by_chip[j] for j in levels[0][1:]]
    body = to_chip(after(placed[2], *first), mid)
    payloads = [placed[0], head, body]
    for value, (j, _, _) in list(zip(placed, parts, strict=True))[3:-1]:
        payloads.append(to_chip(after(value, *first), j))
    for level in levels[1:]:
        for j in level:
            bit = j & -j
            by_chip[j] = to_chip(after(by_chip[j ^ bit], *first), bit)

    buffers, segments = [], []
    for n, level in enumerate(levels):
        held = [by_chip[j] for j in level]
        held = held[0] if len(held) == 1 else jnp.concatenate(held)
        if n == 0:
            held = after(held, *first)
        if n == 1:
            held = after(held, far)
        held = [(held, ((0, 0),))]
        for step in range(steps):
            if n:
                merged = jnp.concatenate([value for value, _ in held]) if step else held[0][0]
                if n == 1 and step == steps - 1:
                    payloads.append(to_chip(after(placed[-1], merged), 1))
                    merged = after(merged, body)
                held = [(merged, sum((origins for _, origins in held), ()))]
            masks = [plane_masks(groups, c)[step] for c in range(CORES)]
            held = held + [
                (in_plane(value, step), tuple((a ^ masks[0], b ^ masks[1]) for a, b in origins))
                for value, origins in held
            ]
        for value, origins in held:
            buffers.append(value)
            segments.append((level, origins))
    sizes = (chips, groups, blocks, relations)
    early = [i for i, (j, _, _) in enumerate(parts) if j in (0, mid)]
    late = [i for i in range(len(parts)) if i not in early][::-1]
    split = sum(level == levels[0] for level, _ in segments)
    inputs, weights = turned(place, near, far, rel_weights)
    adjoint, total = early_tiles(
        tuple(parts[i] for i in early),
        segments[:split],
        after(place, inputs, weights),
        buffers[:split],
        [payloads[i] for i in early],
        sizes,
    )
    rows_far, summed, _ = late_tiles_and_rows(
        tuple(parts[i] for i in late),
        sorted(levels[0]),
        segments[split:],
        place,
        adjoint,
        total,
        buffers[split:],
        [payloads[i] for i in late],
        weights,
        sizes,
    )
    rows_far = across(rows_far, "node", nodes, 1)
    sums, passed = row_terms(place, summed, weights, rows_far)
    for step in range(steps):
        if step:
            half = sums.shape[0] // 2
            sums, passed = sums[:half], sums[half:].astype(jnp.bfloat16)
        sums = sums + in_plane(passed, step).astype(jnp.float32)
    d_source = sums[0] + jnp.einsum(
        "vj,ij->vi", own, self_weight, preferred_element_type=jnp.float32
    )

    grad_far, grad_own = grad_terms(place, summed, inputs, chips)
    grad_far = across(grad_far, "node", nodes, 1)
    grad = grad_own + grad_far.astype(jnp.float32)
    others = [to_chip(grad[j].astype(jnp.bfloat16), j) for j in range(chips - 1, 0, -1)]
    rel_weight_grad = grad[0]
    for other in others:
        rel_weight_grad += other.astype(jnp.float32)
    return rel_weight_grad, d_source.astype(jnp.bfloat16)[None]


def solution(mesh):
    return jax.shard_map(
        on_device,
        mesh=mesh,
        in_specs=(
            P("node", "rel", None),
            P("node", None, None),
            P("rel", None, None),
            P(),
            P("rel", "node", None, None),
            P("rel", "node"),
            P("rel", "node"),
            P("rel", "node"),
            P("rel", "node", None),
        ),
        out_specs=(P("rel", "node", None), P("node", "rel", None)),
        check_vma=False,
    )
```

```python
import functools

import jax
import jax.numpy as jnp
from jax import lax
from jax.experimental import pallas as pl
from jax.experimental.pallas import tpu as pltpu
from jax.sharding import PartitionSpec as P

CAPACITY = 8
CORES = 2
SLOTS = CORES * CAPACITY
LIMIT = 24 * 1024 * 1024
HEAD = 2
SMEM = pl.BlockSpec(memory_space=pltpu.SMEM)
VMEM = pl.BlockSpec(memory_space=pltpu.VMEM)
ANY = pl.BlockSpec(memory_space=pl.ANY)


def payload_rows(edge, first, size):
    return size * edge + (SLOTS if first == 0 else 0)


def place_kernel(parts, chips, blocks, relations, *refs):
    given, place_ref, outs = refs[:2], refs[2], refs[3 : 3 + len(parts)]
    details, tiles_ref, order, count, sem = refs[3 + len(parts) :]
    copies = [
        pltpu.make_async_copy(given[0], details, sem.at[0]),
        pltpu.make_async_copy(given[1], tiles_ref, sem.at[1]),
    ]
    for copy in copies:
        copy.start()
    chip = place_ref[0]
    edge = tiles_ref.shape[-1]
    for j in range(chips):
        count[j] = 0
    for s in range(chips * SLOTS):
        order[s] = 0
    copies[0].wait()

    def rank(t, carry):
        j = (details[0, t] // CORES) ^ chip
        p = count[j]
        order[j * SLOTS + p] = t
        count[j] = p + 1
        return carry

    lax.fori_loop(0, details.shape[1], rank, 0)
    copies[1].wait()
    lane = lax.broadcasted_iota(jnp.int32, (SLOTS, edge), 1)
    row = lax.broadcasted_iota(jnp.int32, (SLOTS, edge), 0)
    for out, (j, first, size) in zip(outs, parts, strict=True):
        for p in range(size):
            tile = tiles_ref[order[j * SLOTS + first + p]]
            full = first + p < count[j]
            out[p * edge : (p + 1) * edge, :] = jnp.where(full, tile, jnp.zeros_like(tile))
        if first == 0:
            codes = jnp.zeros((SLOTS, edge), jnp.int32)
            for p in range(SLOTS):
                t = order[j * SLOTS + p]
                bucket = (details[0, t] % CORES) * relations + details[1, t]
                code = jnp.where(lane == 0, bucket * blocks + details[3, t], details[2, t])
                codes = jnp.where(row == p, code, codes)
            out[size * edge :, :] = codes.astype(jnp.float32).astype(jnp.bfloat16)


def place_tiles(parts, chips, blocks, relations, details, tiles, place):
    edge = tiles.shape[-1]
    shapes = [
        jax.ShapeDtypeStruct((payload_rows(edge, first, size), edge), tiles.dtype)
        for _, first, size in parts
    ]
    return pl.pallas_call(
        functools.partial(place_kernel, parts, chips, blocks, relations),
        out_shape=shapes,
        in_specs=[ANY] * 2 + [SMEM],
        out_specs=[VMEM] * len(shapes),
        scratch_shapes=[
            pltpu.SMEM(details.shape, jnp.int32),
            pltpu.VMEM(tiles.shape, tiles.dtype),
            pltpu.SMEM((chips * SLOTS,), jnp.int32),
            pltpu.SMEM((chips,), jnp.int32),
            pltpu.SemaphoreType.DMA((2,)),
        ],
        compiler_params=pltpu.CompilerParams(vmem_limit_bytes=LIMIT),
        cost_estimate=pl.CostEstimate(flops=0, bytes_accessed=4_000_000, transcendentals=0),
        name="place_tiles",
    )(details, tiles, place)


def read_codes(parts, payloads, vector, codes, sem):
    copies = {}
    for payload, (j, first, size) in zip(payloads, parts, strict=True):
        if first == 0:
            last = payload[payload.shape[0] - SLOTS :, :]
            vector[j] = last.astype(jnp.float32).astype(jnp.int32)
            copies[j] = pltpu.make_async_copy(vector.at[j], codes.at[j], sem.at[j])
            copies[j].start()
    return copies


def gather_moves(buffers, segments, place_ref, groups, adjoint, landed):
    group, core = place_ref[1], place_ref[2]
    piece = adjoint.shape[1] // groups
    where = sorted({j for level, _ in segments for j in level})
    moves = {j: [] for j in where}
    for buffer, (level, origins) in zip(buffers, segments, strict=True):
        for q, origin in enumerate(origins):
            start = jnp.where(core == 0, origin[0], origin[1]) ^ group
            start = pl.multiple_of(start * piece, piece)
            for n, j in enumerate(level):
                moves[j].append(
                    pltpu.make_async_copy(
                        buffer.at[pl.ds((q * len(level) + n) * piece, piece)],
                        adjoint.at[where.index(j), pl.ds(start, piece)],
                        landed.at[where.index(j), len(moves[j])],
                    )
                )
                moves[j][-1].start()
    return where, moves


def add_tiles(payload, j, first, size, adjoint, total, codes):
    edge = payload.shape[-1]
    unroll = next(u for u in range(min(size, 16), 0, -1) if size % u == 0)
    if unroll == 1:
        unroll = size

    def some(i, carry):
        for u in range(unroll):
            p = i * unroll + u
            row = pl.multiple_of(codes[j, first + p, 1] * edge, edge)
            partial = lax.dot_general(
                payload[pl.ds(pl.multiple_of(p * edge, edge), edge), :],
                adjoint[pl.ds(row, edge), :],
                (((0,), (0,)), ((), ())),
                preferred_element_type=jnp.float32,
            )
            total[codes[j, first + p, 0]] += partial.astype(jnp.bfloat16).astype(jnp.float32)
        return carry

    lax.fori_loop(0, size // unroll, some, 0)


def early_kernel(parts, segments, groups, place_ref, *refs):
    buffers, refs = refs[: len(segments)], refs[len(segments) :]
    payloads, refs = refs[: len(parts)], refs[len(parts) :]
    adjoint, total, vector, codes, sem, landed = refs
    where, moves = gather_moves(buffers, segments, place_ref, groups, adjoint, landed)
    copies = read_codes(parts, payloads, vector, codes, sem)
    total[...] = jnp.zeros_like(total)
    for j in where:
        for move in moves[j]:
            move.wait()
    for payload, (j, first, size) in zip(payloads, parts, strict=True):
        if first == 0:
            copies[j].wait()
        add_tiles(payload, j, first, size, adjoint.at[where.index(j)], total, codes)


def early_tiles(parts, segments, place, buffers, payloads, sizes):
    chips, groups, blocks, relations = sizes
    edge, feature = payloads[0].shape[-1], buffers[0].shape[-1]
    held = len({j for level, _ in segments for j in level})
    return pl.pallas_call(
        functools.partial(early_kernel, parts, segments, groups),
        out_shape=[
            jax.ShapeDtypeStruct((held, blocks * edge, feature), jnp.bfloat16),
            jax.ShapeDtypeStruct((CORES * relations * blocks, edge, feature), jnp.float32),
        ],
        in_specs=[SMEM] + [ANY] * len(buffers) + [VMEM] * len(payloads),
        out_specs=[VMEM] * 2,
        scratch_shapes=[
            pltpu.VMEM((chips, SLOTS, edge), jnp.int32),
            pltpu.SMEM((chips, SLOTS, edge), jnp.int32),
            pltpu.SemaphoreType.DMA((chips,)),
            pltpu.SemaphoreType.DMA((held, groups)),
        ],
        compiler_params=pltpu.CompilerParams(vmem_limit_bytes=LIMIT),
        cost_estimate=pl.CostEstimate(flops=0, bytes_accessed=1_000_000, transcendentals=0),
        name="early_tiles",
    )(place, *buffers, *payloads)


def late_kernel(parts, held, segments, sizes, place_ref, adjoint, before, *refs):
    chips, groups, blocks, relations = sizes
    buffers, refs = refs[: len(segments)], refs[len(segments) :]
    payloads, refs = refs[: len(parts)], refs[len(parts) :]
    weights_ref, rows_far, summed, total, late, vector, codes, sem, landed = refs
    edge = payloads[0].shape[-1]
    where, moves = gather_moves(buffers, segments, place_ref, groups, late, landed)
    copies = read_codes(parts, payloads, vector, codes, sem)
    for payload, (j, first, size) in zip(payloads, parts, strict=True):
        if first == 0:
            copies[j].wait()
            for move in moves.get(j, []):
                move.wait()
        shard = late.at[where.index(j)] if j in where else adjoint.at[held.index(j)]
        add_tiles(payload, j, first, size, shard, total, codes)

    for h in range(CORES):
        for r in range(relations):
            part = total[pl.ds((h * relations + r) * blocks, blocks)].astype(jnp.bfloat16)
            part = part.reshape(blocks * edge, part.shape[-1])
            rows, feature = part.shape
            summed[h * rows : (h + 1) * rows, r * feature : (r + 1) * feature] = part
    for spot, value in multiply_rows(place_ref, summed, weights_ref, groups, 1):
        rows_far[spot] = value.astype(rows_far.dtype)


def multiply_rows(place_ref, summed, weights_ref, groups, far):
    group, core = place_ref[1], place_ref[2]
    rows = summed.shape[0] // CORES
    piece = rows // groups
    steps = groups.bit_length() - 1
    value = jnp.dot(
        summed[pl.ds(pl.multiple_of((core ^ far) * rows, rows), rows), :],
        weights_ref[...],
        preferred_element_type=jnp.float32,
    )
    pieces = []
    for q in range(groups):
        mask = group ^ q
        spot = [0, 0]
        for step in range(steps):
            for c in range(CORES):
                bit = plane_masks(groups, c)[step].bit_length() - 1
                spot[c] = spot[c] + (((mask >> bit) & 1) << (steps - 1 - step))
        spot = jnp.where((core ^ far) == 0, spot[0], spot[1])
        pieces.append((spot, value[q * piece : (q + 1) * piece]))
    return pieces


def late_tiles_and_rows(parts, held, segments, place, adjoint, total, buffers, payloads, weights, sizes):
    chips, groups, blocks, relations = sizes
    edge, feature = total.shape[1:]
    rows = blocks * edge
    behind = len({j for level, _ in segments for j in level})
    return pl.pallas_call(
        functools.partial(late_kernel, parts, held, segments, sizes),
        out_shape=[
            jax.ShapeDtypeStruct((groups, rows // groups, feature), jnp.bfloat16),
            jax.ShapeDtypeStruct((CORES * rows, relations * feature), jnp.bfloat16),
            jax.ShapeDtypeStruct(total.shape, total.dtype),
        ],
        in_specs=[SMEM] + [VMEM] * 2 + [ANY] * len(buffers) + [VMEM] * (1 + len(payloads)),
        out_specs=[VMEM] * 3,
        scratch_shapes=[
            pltpu.VMEM((behind, rows, feature), jnp.bfloat16),
            pltpu.VMEM((chips, SLOTS, edge), jnp.int32),
            pltpu.SMEM((chips, SLOTS, edge), jnp.int32),
            pltpu.SemaphoreType.DMA((chips,)),
            pltpu.SemaphoreType.DMA((behind, groups)),
        ],
        input_output_aliases={2: 2},
        compiler_params=pltpu.CompilerParams(vmem_limit_bytes=LIMIT),
        cost_estimate=pl.CostEstimate(flops=0, bytes_accessed=1_000_000, transcendentals=0),
        name="late_tiles_and_rows",
    )(place, adjoint, total, *buffers, *payloads, weights)


def turn_kernel(place_ref, near_ref, far_ref, weights_ref, inputs, weights):
    core = place_ref[2]
    rows, feature = near_ref.shape
    near, far = near_ref[...].T, far_ref[...].T
    for c in range(CORES):

        @pl.when(core == c)
        def _():
            inputs[:, c * rows : (c + 1) * rows] = near
            inputs[:, (1 - c) * rows : (2 - c) * rows] = far

    for r in range(weights_ref.shape[0]):
        weights[r * feature : (r + 1) * feature, :] = weights_ref[r].T


def turned(place, near, far, weights):
    rows, feature = near.shape
    return pl.pallas_call(
        turn_kernel,
        out_shape=[
            jax.ShapeDtypeStruct((feature, CORES * rows), near.dtype),
            jax.ShapeDtypeStruct((weights.shape[0] * feature, feature), weights.dtype),
        ],
        in_specs=[SMEM] + [VMEM] * 3,
        out_specs=[VMEM] * 2,
        compiler_params=pltpu.CompilerParams(vmem_limit_bytes=LIMIT),
        cost_estimate=pl.CostEstimate(flops=0, bytes_accessed=1_000_000, transcendentals=0),
        name="turn_inputs",
    )(place, near, far, weights)


def rows_kernel(groups, place_ref, summed, weights_ref, far_ref, kept, sent):
    half = groups // 2
    for spot, value in multiply_rows(place_ref, summed, weights_ref, groups, 0):
        value += far_ref[spot].astype(jnp.float32)

        @pl.when(spot < half)
        def _():
            kept[spot] = value

        @pl.when(spot >= half)
        def _():
            sent[spot - half] = value.astype(sent.dtype)


def row_terms(place, summed, weights, far):
    groups, piece, feature = far.shape
    shape = (groups // 2, piece, feature)
    return pl.pallas_call(
        functools.partial(rows_kernel, groups),
        out_shape=[
            jax.ShapeDtypeStruct(shape, jnp.float32),
            jax.ShapeDtypeStruct(shape, jnp.bfloat16),
        ],
        in_specs=[SMEM, VMEM, VMEM, VMEM],
        out_specs=[VMEM] * 2,
        compiler_params=pltpu.CompilerParams(vmem_limit_bytes=LIMIT),
        cost_estimate=pl.CostEstimate(
            flops=2 * summed.size * feature, bytes_accessed=4_000_000, transcendentals=0
        ),
        name="row_terms",
    )(place, summed, weights, far)


def grad_kernel(chips, relations, place_ref, summed, inputs_ref, grad_far, grad_own):
    chip, core = place_ref[0], place_ref[2]
    feature = inputs_ref.shape[0]
    share = feature // (chips * CORES)
    grad = jnp.dot(inputs_ref[...], summed[...], preferred_element_type=jnp.float32)
    for r in range(relations):
        for far in range(CORES):
            out = grad_far if far else grad_own
            for c in range(chips):
                for h in range(CORES):
                    start = (c * CORES + h) * share
                    slab = grad[start : start + share, r * feature : (r + 1) * feature]

                    @pl.when(h == (core ^ far))
                    def _():
                        out[chip ^ c, r] = slab.astype(out.dtype)


def grad_terms(place, summed, inputs, chips):
    feature = inputs.shape[0]
    relations = summed.shape[1] // feature
    shape = (chips, relations, feature // (chips * CORES), feature)
    return pl.pallas_call(
        functools.partial(grad_kernel, chips, relations),
        out_shape=[
            jax.ShapeDtypeStruct(shape, jnp.bfloat16),
            jax.ShapeDtypeStruct(shape, jnp.float32),
        ],
        in_specs=[SMEM, VMEM, VMEM],
        out_specs=[VMEM] * 2,
        compiler_params=pltpu.CompilerParams(vmem_limit_bytes=LIMIT),
        cost_estimate=pl.CostEstimate(flops=0, bytes_accessed=1_000_000, transcendentals=0),
        name="grad_terms",
    )(place, summed, inputs)


def plane_masks(groups, core):
    masks = [1 << i for i in range(groups.bit_length() - 1)]
    return masks[::-1] if core % CORES else masks


def after(value, *others):
    return lax.optimization_barrier((value, *others))[0]


def on_device(
    out_adjoint,
    layer_input,
    rel_weights,
    self_weight,
    tile_values,
    tile_rel,
    tile_target,
    tile_src,
    tile_dest,
):
    nodes = lax.axis_size("node")
    groups = lax.axis_size("rel")
    chips = nodes // CORES
    node = lax.axis_index("node")
    group = lax.axis_index("rel")
    chip, core = node // CORES, node % CORES
    edge = tile_values.shape[-1]
    rows = layer_input.shape[1]
    blocks = rows // edge
    relations = rel_weights.shape[0]

    def across(value, axis, size, mask):
        return lax.ppermute(value, axis, [(i, i ^ mask) for i in range(size)])

    def to_chip(value, j):
        return across(value, "node", nodes, CORES * j)

    def in_plane(value, step):
        pairs = []
        for g in range(groups):
            for n in range(nodes):
                mask = plane_masks(groups, n)[step]
                pairs.append((g * nodes + n, (g ^ mask) * nodes + n))
        return lax.ppermute(value, ("rel", "node"), pairs)

    own = out_adjoint[0]
    place = jnp.stack([chip, group, core]).astype(jnp.int32)
    details = jnp.stack([tile_dest[0, :, 0], tile_rel[0], tile_target[0], tile_src[0]])

    levels = [
        [j for j in range(chips) if j.bit_count() == count]
        for count in range(chips.bit_length())
    ]
    levels[:2] = [levels[0] + levels[1]]
    steps = groups.bit_length() - 1
    near = layer_input[0]
    far = across(near, "node", nodes, 1)
    mid = chips // 2
    parts = [(0, 0, SLOTS), (mid, 0, HEAD), (mid, HEAD, SLOTS - HEAD)]
    parts = tuple(parts + [(j, 0, SLOTS) for j in range(chips - 1, 0, -1) if j != mid])
    placed = place_tiles(parts, chips, blocks, relations, details, tile_values[0], place)

    by_chip = {0: own}
    for j in levels[0][1:]:
        by_chip[j] = to_chip(own, j)
    head = to_chip(placed[1], mid)
    first = [head] + [by_chip[j] for j in levels[0][1:]]
    body = to_chip(after(placed[2], *first), mid)
    payloads = [placed[0], head, body]
    for value, (j, _, _) in list(zip(placed, parts, strict=True))[3:-1]:
        payloads.append(to_chip(after(value, *first), j))
    for level in levels[1:]:
        for j in level:
            bit = j & -j
            by_chip[j] = to_chip(after(by_chip[j ^ bit], *first), bit)

    buffers, segments = [], []
    for n, level in enumerate(levels):
        held = [by_chip[j] for j in level]
        held = held[0] if len(held) == 1 else jnp.concatenate(held)
        if n == 0:
            held = after(held, *first)
        if n == 1:
            held = after(held, far)
        held = [(held, ((0, 0),))]
        for step in range(steps):
            if n:
                merged = jnp.concatenate([value for value, _ in held]) if step else held[0][0]
                if n == 1 and step == steps - 1:
                    payloads.append(to_chip(after(placed[-1], merged), 1))
                    merged = after(merged, body)
                held = [(merged, sum((origins for _, origins in held), ()))]
            masks = [plane_masks(groups, c)[step] for c in range(CORES)]
            held = held + [
                (in_plane(value, step), tuple((a ^ masks[0], b ^ masks[1]) for a, b in origins))
                for value, origins in held
            ]
        for value, origins in held:
            buffers.append(value)
            segments.append((level, origins))
    sizes = (chips, groups, blocks, relations)
    early = [i for i, (j, _, _) in enumerate(parts) if j in (0, mid)]
    late = [i for i in range(len(parts)) if i not in early][::-1]
    split = sum(level == levels[0] for level, _ in segments)
    inputs, weights = turned(place, near, far, rel_weights)
    adjoint, total = early_tiles(
        tuple(parts[i] for i in early),
        segments[:split],
        after(place, inputs, weights),
        buffers[:split],
        [payloads[i] for i in early],
        sizes,
    )
    rows_far, summed, _ = late_tiles_and_rows(
        tuple(parts[i] for i in late),
        sorted(levels[0]),
        segments[split:],
        place,
        adjoint,
        total,
        buffers[split:],
        [payloads[i] for i in late],
        weights,
        sizes,
    )
    rows_far = across(rows_far, "node", nodes, 1)
    sums, passed = row_terms(place, summed, weights, rows_far)
    for step in range(steps):
        if step:
            half = sums.shape[0] // 2
            sums, passed = sums[:half], sums[half:].astype(jnp.bfloat16)
        sums = sums + in_plane(passed, step).astype(jnp.float32)
    d_source = sums[0] + jnp.einsum(
        "vj,ij->vi", own, self_weight, preferred_element_type=jnp.float32
    )

    grad_far, grad_own = grad_terms(place, summed, inputs, chips)
    grad_far = across(grad_far, "node", nodes, 1)
    grad = grad_own + grad_far.astype(jnp.float32)
    others = [to_chip(grad[j].astype(jnp.bfloat16), j) for j in range(chips - 1, 0, -1)]
    rel_weight_grad = grad[0]
    for other in others:
        rel_weight_grad += other.astype(jnp.float32)
    return rel_weight_grad, d_source.astype(jnp.bfloat16)[None]


def solution(mesh):
    return jax.shard_map(
        on_device,
        mesh=mesh,
        in_specs=(
            P("node", "rel", None),
            P("node", None, None),
            P("rel", None, None),
            P(),
            P("rel", "node", None, None),
            P("rel", "node"),
            P("rel", "node"),
            P("rel", "node"),
            P("rel", "node", None),
        ),
        out_specs=(P("rel", "node", None), P("node", "rel", None)),
        check_vma=False,
    )
```
